32 devices in a mesh: group: 2 (over y), tok: 8 (over z, x), col: 2 (over core).
Axes of the slice: x: 2, y: 2, z: 4, core: 2. Of those that a mesh axis runs over, the one named last changes fastest.
Arguments:
- hidden: bfloat16 [8192, 8192], P(('group', 'tok', 'col')), parts along dimension 0, may hold values from -120 to 120
- gain_table: bfloat16 [80, 8192], P(None, 'tok'), may hold values from 0.099609375 to 1.8984375
- layer_id: int32 [2], P('group'), parts along dimension 0, may hold values from 0 to 79
- w_key: bfloat16 [8192, 512], P('tok', 'col'), may hold values from -0.0625 to 0.0625
- w_value: bfloat16 [8192, 512], P('tok', 'col'), may hold values from -0.0625 to 0.0625
- offsets: int32 [16], P(('group', 'tok')), parts along dimension 0, may hold values from 0 to 130559
- owner_map: int32 [16], P('group'), parts along dimension 0, may hold values from 0 to 7, each once
Outputs:
- key_cache: bfloat16 [2, 16384, 128], P('col', ('group', 'tok')), parts along dimension 1
- value_cache: bfloat16 [2, 16384, 128], P('col', ('group', 'tok')), parts along dimension 1
The draws below stay inside these ranges and needn't reach their ends.
There are 2 independent parts, one for each index of `group`. The reference program is written for one: setup_inputs(seed, part) draws one part's arguments, and reference() takes and returns one part's arrays. A program takes and returns all parts, laid end to end along the dimension named above; an argument that names none is the same for every part. Nothing has to cross between parts.
Inputs may be any that keep to these rules, and one draw needn't show every extreme that they name: `owner_map`: each tok index owns exactly one group.
All inputs are finite; a program needn't handle non-finite values.
Results may differ from the reference program's by a relative error of at most 0.006.
Values may be sent and summed in bfloat16 or wider, within the bound.
No kernel may reach another device: no remote copies, remote signals or barrier semaphores. Data moves between devices by JAX's collectives and lax.ppermute only.
A program may use at most 64 MiB of HBM per device.

```python
import math
import jax
import jax.numpy as jnp
from jax import lax

D = 8192
HD = 128
LAYERS_ALL = 80
KVH = 4
TOK_DEV = 512
TOKENS = 4096
N_TOK = 8
N_COL = 2


def draw_hidden(key, part):
    key = jax.random.fold_in(key, 11)
    base_key, row_key, col_key = jax.random.split(key, 3)
    row_scale = jnp.exp(jax.random.uniform(row_key, (TOKENS, 1), jnp.float32, 0.0, math.log(10.0)))
    col_scale = jnp.exp(jax.random.uniform(col_key, (1, D), jnp.float32, -math.log(3.0), math.log(3.0)))
    base = jax.random.normal(base_key, (TOKENS, D), jnp.float32)
    base = jnp.clip(base, -4.0, 4.0)
    return (base * row_scale * col_scale).astype(jnp.bfloat16)


def touch_ends(result, rng, least, high):
    longest = result.shape.index(max(result.shape))
    spots = []
    for shift in (0, 1):
        where = [jax.random.randint(jax.random.fold_in(rng, axis), (), 0, length) for axis, length in enumerate(result.shape)]
        where[longest] = (where[longest] + shift) % result.shape[longest]
        spots.append(tuple(where))
    return result.at[spots[0]].set(least).at[spots[1]].set(high)


def block_levels(own_key, extent, cuts, smallest, top_value):
    level = 1.0
    for dim, blocks in cuts:
        steps = jax.random.uniform(jax.random.fold_in(jax.random.fold_in(own_key, 6), dim), (blocks,), jnp.float32, smallest / len(cuts), top_value / len(cuts))
        level = level * jnp.repeat(jnp.exp(steps), extent[dim] // blocks).reshape((-1,) + (1,) * (len(extent) - 1 - dim))
    return level


def gaussian(own_key, shape, scale, reach, cuts=(), held_as=jnp.bfloat16):
    values = jax.random.normal(own_key, shape, jnp.float32) * scale
    if len(cuts) > 0:
        values = block_levels(own_key, shape, cuts, -0.22, 0.18) * values
    return jnp.clip(values, min=-reach, max=reach).astype(held_as)


def setup_inputs(seed: int = 0, part: int = 0) -> dict:
    streams_of = jax.random.split(jax.random.key(seed), 8)
    part_splits = jax.random.split(jax.random.fold_in(streams_of[7], part), 8)
    return {
        "hidden": draw_hidden(jax.random.fold_in(jax.random.fold_in(streams_of[7], part), 71), part),
        "gain_table": jnp.clip(1.0 + 0.18 * jax.random.normal(streams_of[1], (LAYERS_ALL, D), jnp.float32), 0.099609375, 1.8984375).astype(jnp.bfloat16),
        "layer_id": jax.random.randint(part_splits[2], (1,), 0, LAYERS_ALL).astype(jnp.int32),
        "w_key": gaussian(streams_of[3], (D, KVH * HD), D ** -0.5, 0.0625, ((0, 8), (1, 2))),
        "w_value": gaussian(streams_of[4], (D, KVH * HD), D ** -0.5, 0.0625, ((0, 8), (1, 2))),
        "offsets": touch_ends(jax.random.randint(part_splits[5], (N_TOK,), 0, 131072 - TOK_DEV), jax.random.fold_in(part_splits[5], 1), 0, (131072 - TOK_DEV) - 1).astype(jnp.int32),
        "owner_map": jax.random.permutation(part_splits[6], N_TOK).astype(jnp.int32),
    }


def rotate(unrotated, position):
    size_head = unrotated.shape[-1]
    half_size = size_head // 2
    frequency = jnp.power(jnp.float32(500000.0), -2.0 * jnp.arange(half_size, dtype=jnp.float32) / size_head)
    angle = jnp.mod(position.astype(jnp.float32)[:, None] * frequency[None, :], 2.0 * math.pi)
    cosine = jnp.cos(angle)[:, None, :]
    sine = jnp.sin(angle)[:, None, :]
    values = unrotated.astype(jnp.float32)
    first = values[..., :half_size]
    second = values[..., half_size:]
    return jnp.concatenate([first * cosine - second * sine, second * cosine + first * sine], axis=-1).astype(jnp.bfloat16)

def normalize(values, squares_total, gain, feature_count):
    scale = lax.rsqrt(squares_total / feature_count + 1e-05)
    return (values.astype(jnp.float32) * scale[:, None] * gain.astype(jnp.float32)[None, :]).astype(jnp.bfloat16)

def reference(hidden, gain_table, layer_id, w_key, w_value, offsets, owner_map):
    gain = lax.dynamic_index_in_dim(gain_table, layer_id[0], 0, keepdims=False)
    key_weight = w_key.astype(jnp.float32)
    value_weight = w_value.astype(jnp.float32)
    blocks = hidden.reshape(N_TOK, TOK_DEV, D)

    def one_block(block_args):
        rows, start = block_args
        wide = rows.astype(jnp.float32)
        normed = normalize(rows, lax.optimization_barrier(jnp.sum(wide * wide, axis=1)), gain, D).astype(jnp.float32)
        key_raw = jnp.dot(normed, key_weight, precision=lax.Precision.HIGHEST).astype(jnp.bfloat16)
        value_raw = jnp.dot(normed, value_weight, precision=lax.Precision.HIGHEST).astype(jnp.bfloat16)
        position = start + jnp.arange(TOK_DEV, dtype=jnp.int32)
        key_rot = rotate(key_raw.reshape(TOK_DEV, KVH, HD), position)
        return (key_rot, value_raw.reshape(TOK_DEV, KVH, HD))
    keys, values = lax.map(one_block, (blocks, offsets))
    per_col = KVH // N_COL
    classes = N_TOK // per_col
    page = TOK_DEV // classes
    group_ids = jnp.arange(N_TOK, dtype=jnp.int32)
    inverse = jnp.zeros((N_TOK,), jnp.int32).at[owner_map].set(group_ids)

    def layout(array):
        grouped = array.reshape(N_TOK, classes, page, N_COL, per_col, HD).transpose(3, 4, 1, 0, 2, 5)
        grouped = grouped.reshape(N_COL, per_col * classes, N_TOK * page, HD)
        return jnp.take(grouped, inverse, axis=1).reshape(N_COL, per_col * classes * N_TOK * page, HD)
    return (layout(keys), layout(values))
```

```python
import functools
import math

import jax
import jax.numpy as jnp
from jax import lax
from jax.experimental import pallas as pl
from jax.experimental.pallas import tpu as pltpu
from jax.sharding import PartitionSpec as P

HD = 128
GAIN_ROWS = 16
VMEM_LIMIT = 56 * 2**20


def rotary_table(position, size_head):
    half_size = size_head // 2
    frequency = jnp.power(
        jnp.float32(500000.0), -2.0 * jnp.arange(half_size, dtype=jnp.float32) / size_head
    )
    angle = jnp.mod(position.astype(jnp.float32)[:, None] * frequency[None, :], 2.0 * math.pi)
    return jnp.cos(angle), jnp.sin(angle)


def rotate(unrotated, position):
    half_size = unrotated.shape[-1] // 2
    cosine, sine = rotary_table(position, unrotated.shape[-1])
    cosine, sine = cosine[:, None, :], sine[:, None, :]
    values = unrotated.astype(jnp.float32)
    first = values[..., :half_size]
    second = values[..., half_size:]
    return jnp.concatenate(
        [first * cosine - second * sine, second * cosine + first * sine], axis=-1
    ).astype(jnp.bfloat16)


def normalize(values, squares_total, gain, feature_count):
    scale = lax.rsqrt(squares_total / feature_count + 1e-05)
    return (values.astype(jnp.float32) * scale[:, None] * gain.astype(jnp.float32)[None, :]).astype(
        jnp.bfloat16
    )


def general_shards(hidden, gain_table, layer_id, w_key, w_value, offsets, owner_map):
    tok_count = lax.axis_size("tok")
    col_count = lax.axis_size("col")
    gain_piece = lax.dynamic_index_in_dim(gain_table, layer_id[0], 0, keepdims=False)
    gain_full = lax.all_gather(gain_piece, "tok", axis=0, tiled=True)
    feature_count = gain_full.shape[0]
    block_rows = hidden.shape[0] * col_count
    tok_rows = lax.all_gather(hidden, "col", axis=0, tiled=True)
    wide = tok_rows.astype(jnp.float32)
    normed = normalize(tok_rows, jnp.sum(wide * wide, axis=1), gain_full, feature_count)
    key_raw, value_new = (
        jnp.dot(
            normed,
            lax.all_gather(weight, "tok", axis=0, tiled=True),
            preferred_element_type=jnp.float32,
        ).astype(jnp.bfloat16)
        for weight in (w_key, w_value)
    )
    heads_here = key_raw.shape[1] // HD
    classes = tok_count // heads_here
    page = block_rows // classes
    group_ids = jnp.arange(tok_count, dtype=jnp.int32)
    inverse = jnp.zeros((tok_count,), jnp.int32).at[owner_map].set(group_ids)

    def arrange_pages(values):
        grouped = (
            values.reshape(classes, page, heads_here, HD)
            .transpose(2, 0, 1, 3)
            .reshape(tok_count, page, HD)
        )
        return jnp.take(grouped, inverse, axis=0).reshape(tok_count * page, HD)

    position = offsets[0] + jnp.arange(block_rows, dtype=jnp.int32)
    key_new = rotate(key_raw.reshape(block_rows, heads_here, HD), position).reshape(block_rows, -1)
    key_out, value_out = (
        lax.all_to_all(arrange_pages(values), "tok", split_axis=0, concat_axis=0, tiled=True)
        for values in (key_new, value_new)
    )
    return (key_out.reshape(1, -1, HD), value_out.reshape(1, -1, HD))


def half_kernel(parity_ref, hidden_ref, half_ref):
    half_ref[...] = hidden_ref[...]


def feature_half(hidden, parity, shard, row_block, rows):
    count = hidden.shape[1] // shard // 2
    return pl.pallas_call(
        half_kernel,
        grid_spec=pltpu.PrefetchScalarGridSpec(
            num_scalar_prefetch=1,
            grid=(count,),
            in_specs=[pl.BlockSpec((rows, shard), lambda i, par: (row_block, 2 * i + par[0]))],
            out_specs=pl.BlockSpec((rows, shard), lambda i, par: (0, i)),
        ),
        out_shape=jax.ShapeDtypeStruct((rows, count * shard), hidden.dtype),
    )(parity, hidden)


def pack_kernel(scalars_ref, key_ref, value_ref, gain_ref, *piece_refs):
    rows = piece_refs[0].shape[0] - GAIN_ROWS
    columns = key_ref.shape[1]
    width = 2 * columns
    table = gain_ref[...].astype(jnp.float32)
    pick = lax.broadcasted_iota(jnp.int32, table.shape, 0) == scalars_ref[1]
    gain = jnp.sum(jnp.where(pick, table, 0.0), axis=0, keepdims=True)
    for p, piece_ref in enumerate(piece_refs):
        piece_ref[:rows, :columns] = key_ref[p * rows : (p + 1) * rows, :]
        piece_ref[:rows, columns:] = value_ref[p * rows : (p + 1) * rows, :]
        piece_ref[rows:, :] = jnp.broadcast_to(
            gain[:, p * width : (p + 1) * width], (GAIN_ROWS, width)
        ).astype(piece_ref.dtype)


def pack_weights(w_key, w_value, gain_table, group_index, layer, pieces):
    shard, columns = w_key.shape
    half = shard // 2
    rows = half // pieces
    return pl.pallas_call(
        pack_kernel,
        grid_spec=pltpu.PrefetchScalarGridSpec(
            num_scalar_prefetch=1,
            grid=(1,),
            in_specs=[
                pl.BlockSpec((half, columns), lambda i, s: (s[0], 0)),
                pl.BlockSpec((half, columns), lambda i, s: (s[0], 0)),
                pl.BlockSpec(gain_table.shape, lambda i, s: (0, 0)),
            ],
            out_specs=[
                pl.BlockSpec((rows + GAIN_ROWS, 2 * columns), lambda i, s: (0, 0))
                for _ in range(pieces)
            ],
        ),
        out_shape=[
            jax.ShapeDtypeStruct((rows + GAIN_ROWS, 2 * columns), w_key.dtype)
            for _ in range(pieces)
        ],
    )(jnp.stack([group_index, layer]), w_key, w_value, gain_table)


def multiply_kernel(line, pieces, shard, *refs):
    refs = list(refs)
    scalars_ref = refs.pop(0)
    own_ref, other_ref = refs.pop(0), refs.pop(0)
    own_pair = [refs.pop(0) for _ in range(2)]
    other_pair = [refs.pop(0) for _ in range(2)]
    scale_ref, key_ref, value_ref = refs.pop(0), refs.pop(0), refs.pop(0)
    mine = [[refs.pop(0) for _ in range(pieces)] for _ in range(line)]
    theirs = [None] + [[refs.pop(0) for _ in range(pieces)] for _ in range(line - 1)]
    key_keep, key_send, value_keep, value_send, weights, gains, rows_ref = refs
    y, x, z, c = (scalars_ref[i] for i in range(4))
    columns = key_ref.shape[1]
    width = 2 * columns
    half = shard // 2
    rows = half // pieces
    for d in range(line):
        base = jnp.bitwise_xor(z, d) * shard
        for p in range(pieces):
            gain = mine[d][p][rows : rows + 8, :].astype(jnp.float32)
            gains[:, pl.ds(pl.multiple_of(base + p * width, 128), width)] = gain
        if d == 0:
            start = pl.multiple_of(base, shard)
            weights[pl.ds(start, shard), :columns] = key_ref[...]
            weights[pl.ds(start, shard), columns:] = value_ref[...]
            continue
        for blocks, side in ((mine[d], y), (theirs[d], 1 - y)):
            for p in range(pieces):
                start = pl.multiple_of(base + side * half + p * rows, rows)
                weights[pl.ds(start, rows), :] = blocks[p][:rows, :]
    page = own_ref.shape[0] // 2
    for pair_side in range(2):
        for core_side in range(2):
            for i in range(line):
                lanes = pl.ds(i * shard, shard)
                gain = gains[0:1, lanes]
                if pair_side == 0:
                    source = (own_ref, other_ref)[core_side]
                    picked = pl.ds(pl.multiple_of((2 * i + x) * shard, shard), shard)
                    rows_ref[:, lanes] = (source[:, picked].astype(jnp.float32) * gain).astype(
                        jnp.bfloat16
                    )
                else:
                    for chunk in range(2):
                        source = (own_pair, other_pair)[core_side][chunk]
                        rows_ref[chunk * page : (chunk + 1) * page, lanes] = (
                            source[:, lanes].astype(jnp.float32) * gain
                        ).astype(jnp.bfloat16)
            product = jnp.dot(rows_ref[...], weights[...], preferred_element_type=jnp.float32)
            scale = scale_ref[pair_side * 2 + core_side]
            source_x = jnp.bitwise_xor(x, pair_side)
            core = jnp.bitwise_xor(c, core_side)
            for j in range(columns // HD):
                for part in range(2):
                    group = j * 4 + core * 2 + part
                    owner = scalars_ref[4 + group]
                    owner_z, owner_x = owner // 2, owner % 2
                    page_rows = slice(part * page, (part + 1) * page)
                    results = [
                        product[page_rows, k * columns + j * HD : k * columns + (j + 1) * HD]
                        * scale[page_rows, :]
                        for k in range(2)
                    ]

                    @pl.when(owner_x == x)
                    def _():
                        key_keep[owner_z, source_x] = results[0]
                        value_keep[owner_z, source_x] = results[1]

                    @pl.when(owner_x != x)
                    def _():
                        key_send[owner_z, source_x] = results[0].astype(jnp.bfloat16)
                        value_send[owner_z, source_x] = results[1].astype(jnp.bfloat16)


def multiply(scalars, own, other, own_pair, other_pair, scale, w_key, w_value, mine, theirs):
    line, pieces = len(mine), len(mine[0])
    shard, columns = w_key.shape
    page = own.shape[0] // 2
    operands = [
        own, other, *own_pair, *other_pair, scale, w_key, w_value,
        *[piece for blocks in mine for piece in blocks],
        *[piece for blocks in theirs[1:] for piece in blocks],
    ]
    vmem = pl.BlockSpec(memory_space=pltpu.VMEM)
    keep = jax.ShapeDtypeStruct((line, 2, page, HD), jnp.float32)
    send = jax.ShapeDtypeStruct((line, 2, page, HD), jnp.bfloat16)
    features = line * shard
    return pl.pallas_call(
        functools.partial(multiply_kernel, line, pieces, shard),
        in_specs=[pl.BlockSpec(memory_space=pltpu.SMEM)] + [vmem] * len(operands),
        out_specs=[vmem] * 4,
        out_shape=[keep, send, keep, send],
        scratch_shapes=[
            pltpu.VMEM((features, 2 * columns), jnp.bfloat16),
            pltpu.VMEM((8, features), jnp.float32),
            pltpu.VMEM((2 * page, features), jnp.bfloat16),
        ],
        compiler_params=pltpu.CompilerParams(vmem_limit_bytes=VMEM_LIMIT),
    )(scalars, *operands)


def finish_key_kernel(scalars_ref, keep_ref, came_ref, cos_ref, sin_ref, *out_refs):
    x, z = scalars_ref[1], scalars_ref[2]
    page = keep_ref.shape[2]
    for d, out_ref in enumerate(out_refs):
        owner_z = jnp.bitwise_xor(z, d)
        owner = owner_z * 2 + x
        group = jnp.int32(0)
        for g in range(2 * len(out_refs)):
            group = jnp.where(scalars_ref[4 + g] == owner, g, group)
        page_class = group % 4
        for s in range(2):
            raw = keep_ref[owner_z, s] + came_ref[owner_z, s].astype(jnp.float32)
            raw = raw.astype(jnp.bfloat16).astype(jnp.float32)
            turned = pltpu.roll(raw, HD // 2, 1)
            rotated = raw * cos_ref[s * 4 + page_class] + turned * sin_ref[s * 4 + page_class]
            out_ref[s * page : (s + 1) * page, :] = rotated.astype(jnp.bfloat16)


def finish_value_kernel(scalars_ref, keep_ref, came_ref, *out_refs):
    z = scalars_ref[2]
    page = keep_ref.shape[2]
    for d, out_ref in enumerate(out_refs):
        owner_z = jnp.bitwise_xor(z, d)
        for s in range(2):
            raw = keep_ref[owner_z, s] + came_ref[owner_z, s].astype(jnp.float32)
            out_ref[s * page : (s + 1) * page, :] = raw.astype(jnp.bfloat16)


def finish(kernel, scalars, keep, came, *tables):
    vmem = pl.BlockSpec(memory_space=pltpu.VMEM)
    line, _, page, _ = keep.shape
    return pl.pallas_call(
        kernel,
        in_specs=[pl.BlockSpec(memory_space=pltpu.SMEM)] + [vmem] * (2 + len(tables)),
        out_specs=[vmem] * line,
        out_shape=[jax.ShapeDtypeStruct((2 * page, HD), jnp.bfloat16)] * line,
        compiler_params=pltpu.CompilerParams(vmem_limit_bytes=VMEM_LIMIT),
    )(scalars, keep, came, *tables)


def place_kernel(scalars_ref, *refs):
    out_ref = refs[-1]
    z = scalars_ref[2]
    rows = refs[0].shape[0]
    for d, block_ref in enumerate(refs[:-1]):
        start = pl.multiple_of(jnp.bitwise_xor(z, d) * rows, rows)
        out_ref[pl.ds(start, rows), :] = block_ref[...]


def place(scalars, blocks):
    vmem = pl.BlockSpec(memory_space=pltpu.VMEM)
    return pl.pallas_call(
        place_kernel,
        in_specs=[pl.BlockSpec(memory_space=pltpu.SMEM)] + [vmem] * len(blocks),
        out_specs=vmem,
        out_shape=jax.ShapeDtypeStruct((len(blocks) * blocks[0].shape[0], HD), jnp.bfloat16),
    )(scalars, *blocks)


def paired_shards(hidden, gain_table, layer_id, w_key, w_value, offsets, owner_map):
    tok_count = lax.axis_size("tok")
    line = tok_count // 2
    pieces = 2
    y, tok, c = lax.axis_index("group"), lax.axis_index("tok"), lax.axis_index("col")
    x, z = tok % 2, tok // 2
    shard = w_key.shape[0]
    device_rows = hidden.shape[0]
    scalars = jnp.concatenate([jnp.stack([y, x, z, c]).astype(jnp.int32), owner_map])

    def over_x(values):
        return lax.ppermute(values, "tok", [(t, t ^ 1) for t in range(tok_count)])

    def over_z(values, distance):
        return lax.ppermute(values, "tok", [(t, t ^ (2 * distance)) for t in range(tok_count)])

    def over_y(values):
        return lax.ppermute(values, "group", [(0, 1), (1, 0)])

    def over_c(values):
        return lax.ppermute(values, "col", [(0, 1), (1, 0)])

    chunk = device_rows // 2
    away = jnp.reshape(1 - x, (1,)).astype(jnp.int32)
    own_pair = [over_x(feature_half(hidden, away, shard, i, chunk)) for i in range(2)]
    packed = pack_weights(w_key, w_value, gain_table, y.astype(jnp.int32), layer_id[0], pieces)
    mine = [packed, None, None, None]
    mine[2] = [over_z(piece, 2) for piece in packed]
    mine[1] = [over_z(piece, 1) for piece in packed]
    other = over_c(hidden)
    mine[3] = [over_z(piece, 1) for piece in mine[2]]
    theirs = [None] + [[over_y(piece) for piece in blocks] for blocks in mine[1:]]
    other_pair = [over_c(values) for values in own_pair]

    def squares(values):
        wide = values.astype(jnp.float32)
        return jnp.sum(wide * wide, axis=1)

    facts = jnp.stack(
        [
            jnp.concatenate([squares(hidden), squares(other)]),
            jnp.broadcast_to(offsets[0].astype(jnp.float32), (2 * device_rows,)),
        ]
    )
    pair_facts = over_x(facts)
    totals = jnp.concatenate([facts[0], pair_facts[0]])
    scale = lax.rsqrt(totals / hidden.shape[1] + 1e-05).reshape(4, device_rows, 1)
    scale = jnp.broadcast_to(scale, (4, device_rows, HD))
    starts = jnp.stack([facts[1, 0], pair_facts[1, 0]]).astype(jnp.int32)
    starts = jnp.where(x == 0, starts, starts[::-1])
    block = jnp.arange(2 * device_rows, dtype=jnp.int32)
    cosine, sine = rotary_table((starts[:, None] + block[None, :]).reshape(-1), HD)
    cosine = jnp.concatenate([cosine, cosine], axis=1).reshape(8, chunk, HD)
    sine = jnp.concatenate([-sine, sine], axis=1).reshape(8, chunk, HD)

    key_keep, key_send, value_keep, value_send = multiply(
        scalars, hidden, other, own_pair, other_pair, scale, w_key, w_value, mine, theirs
    )
    key_came, value_came = over_x(key_send), over_x(value_send)
    keys = finish(finish_key_kernel, scalars, key_keep, key_came, cosine, sine)
    values = finish(finish_value_kernel, scalars, value_keep, value_came)
    outs = []
    for blocks in (keys, values):
        blocks = [blocks[0]] + [over_z(blocks[d], d) for d in range(1, line)]
        outs.append(place(scalars, blocks)[None])
    return tuple(outs)


def solution(mesh):
    in_specs = (
        P(("group", "tok", "col"), None),
        P(None, "tok"),
        P("group"),
        P("tok", "col"),
        P("tok", "col"),
        P(("group", "tok")),
        P("group"),
    )
    out_specs = (P("col", ("group", "tok"), None), P("col", ("group", "tok"), None))
    paired = mesh.shape["group"] == 2 and mesh.shape["tok"] == 8 and mesh.shape["col"] == 2
    shards = paired_shards if paired else general_shards
    return jax.shard_map(shards, mesh=mesh, in_specs=in_specs, out_specs=out_specs, check_vma=False)
```

```python
import functools
import math

import jax
import jax.numpy as jnp
from jax import lax
from jax.experimental import pallas as pl
from jax.experimental.pallas import tpu as pltpu
from jax.sharding import PartitionSpec as P

HD = 128
GAIN_ROWS = 16
VMEM_LIMIT = 58 * 2**20
SMALL_VMEM_LIMIT = 8 * 2**20


def rotary_table(position, size_head):
    half_size = size_head // 2
    frequency = jnp.power(
        jnp.float32(500000.0), -2.0 * jnp.arange(half_size, dtype=jnp.float32) / size_head
    )
    angle = jnp.mod(position.astype(jnp.float32)[:, None] * frequency[None, :], 2.0 * math.pi)
    return jnp.cos(angle), jnp.sin(angle)


def rotate(unrotated, position):
    half_size = unrotated.shape[-1] // 2
    cosine, sine = rotary_table(position, unrotated.shape[-1])
    cosine, sine = cosine[:, None, :], sine[:, None, :]
    values = unrotated.astype(jnp.float32)
    first = values[..., :half_size]
    second = values[..., half_size:]
    return jnp.concatenate(
        [first * cosine - second * sine, second * cosine + first * sine], axis=-1
    ).astype(jnp.bfloat16)


def normalize(values, squares_total, gain, feature_count):
    scale = lax.rsqrt(squares_total / feature_count + 1e-05)
    return (values.astype(jnp.float32) * scale[:, None] * gain.astype(jnp.float32)[None, :]).astype(
        jnp.bfloat16
    )


def general_shards(hidden, gain_table, layer_id, w_key, w_value, offsets, owner_map):
    tok_count = lax.axis_size("tok")
    col_count = lax.axis_size("col")
    gain_piece = lax.dynamic_index_in_dim(gain_table, layer_id[0], 0, keepdims=False)
    gain_full = lax.all_gather(gain_piece, "tok", axis=0, tiled=True)
    feature_count = gain_full.shape[0]
    block_rows = hidden.shape[0] * col_count
    tok_rows = lax.all_gather(hidden, "col", axis=0, tiled=True)
    wide = tok_rows.astype(jnp.float32)
    normed = normalize(tok_rows, jnp.sum(wide * wide, axis=1), gain_full, feature_count)
    key_raw, value_new = (
        jnp.dot(
            normed,
            lax.all_gather(weight, "tok", axis=0, tiled=True),
            preferred_element_type=jnp.float32,
        ).astype(jnp.bfloat16)
        for weight in (w_key, w_value)
    )
    heads_here = key_raw.shape[1] // HD
    classes = tok_count // heads_here
    page = block_rows // classes
    group_ids = jnp.arange(tok_count, dtype=jnp.int32)
    inverse = jnp.zeros((tok_count,), jnp.int32).at[owner_map].set(group_ids)

    def arrange_pages(values):
        grouped = (
            values.reshape(classes, page, heads_here, HD)
            .transpose(2, 0, 1, 3)
            .reshape(tok_count, page, HD)
        )
        return jnp.take(grouped, inverse, axis=0).reshape(tok_count * page, HD)

    position = offsets[0] + jnp.arange(block_rows, dtype=jnp.int32)
    key_new = rotate(key_raw.reshape(block_rows, heads_here, HD), position).reshape(block_rows, -1)
    key_out, value_out = (
        lax.all_to_all(arrange_pages(values), "tok", split_axis=0, concat_axis=0, tiled=True)
        for values in (key_new, value_new)
    )
    return (key_out.reshape(1, -1, HD), value_out.reshape(1, -1, HD))


def run_copies(pairs, sems):
    copies = [
        pltpu.make_async_copy(source, target, sems.at[i])
        for i, (source, target) in enumerate(pairs)
    ]
    for copy in copies:
        copy.start()
    return copies


def wait_all(copies):
    for copy in copies:
        copy.wait()


SMEM = pl.BlockSpec(memory_space=pltpu.SMEM)
VMEM = pl.BlockSpec(memory_space=pltpu.VMEM)
HBM = pl.BlockSpec(memory_space=pltpu.HBM)


def half_kernel(shard, parity_ref, hidden_ref, *refs):
    half_refs, sems = refs[:-1], refs[-1]
    pairs = []
    first = 0
    for half_ref in half_refs:
        rows = half_ref.shape[0]
        for i in range(half_ref.shape[1] // shard):
            lanes = pl.ds(pl.multiple_of((2 * i + parity_ref[0]) * shard, shard), shard)
            pairs.append(
                (hidden_ref.at[pl.ds(first, rows), lanes], half_ref.at[:, pl.ds(i * shard, shard)])
            )
        first += rows
    wait_all(run_copies(pairs, sems))


def feature_half(hidden, parity, shard, chunks):
    count = hidden.shape[1] // shard // 2
    return pl.pallas_call(
        functools.partial(half_kernel, shard),
        in_specs=[SMEM, HBM],
        out_specs=[VMEM for _ in chunks],
        out_shape=[jax.ShapeDtypeStruct((rows, count * shard), hidden.dtype) for rows in chunks],
        scratch_shapes=[pltpu.SemaphoreType.DMA((count * len(chunks),))],
    )(parity, hidden)


def pack_kernel(scalars_ref, layer_ref, key_ref, value_ref, gain_ref, *refs):
    *piece_refs, table, sems = refs
    rows = piece_refs[0].shape[0] - GAIN_ROWS
    columns = key_ref.shape[1]
    width = 2 * columns
    layer = layer_ref[0]
    block = pl.multiple_of(layer // GAIN_ROWS * GAIN_ROWS, GAIN_ROWS)
    pairs = [(gain_ref.at[pl.ds(block, GAIN_ROWS), :], table)]
    for p, piece_ref in enumerate(piece_refs):
        first = (scalars_ref[0] * len(piece_refs) + p) * rows
        picked = pl.ds(pl.multiple_of(first, rows), rows)
        for k, weight_ref in enumerate((key_ref, value_ref)):
            pairs.append(
                (
                    weight_ref.at[picked, :],
                    piece_ref.at[pl.ds(0, rows), pl.ds(k * columns, columns)],
                )
            )
    copies = run_copies(pairs, sems)
    copies[0].wait()
    found = table[...].astype(jnp.float32)
    pick = lax.broadcasted_iota(jnp.int32, found.shape, 0) == layer % GAIN_ROWS
    gain = jnp.sum(jnp.where(pick, found, 0.0), axis=0, keepdims=True)
    for p, piece_ref in enumerate(piece_refs):
        piece_ref[rows:, :] = jnp.broadcast_to(
            gain[:, p * width : (p + 1) * width], (GAIN_ROWS, width)
        ).astype(piece_ref.dtype)
    wait_all(copies[1:])


def pack_weights(scalars, layer_id, w_key, w_value, gain_table, pieces):
    shard, columns = w_key.shape
    rows = shard // 2 // pieces
    piece = jax.ShapeDtypeStruct((rows + GAIN_ROWS, 2 * columns), w_key.dtype)
    return pl.pallas_call(
        pack_kernel,
        in_specs=[SMEM, SMEM, HBM, HBM, HBM],
        out_specs=[VMEM] * pieces,
        out_shape=[piece] * pieces,
        scratch_shapes=[
            pltpu.VMEM((GAIN_ROWS, gain_table.shape[1]), gain_table.dtype),
            pltpu.SemaphoreType.DMA((1 + 2 * pieces,)),
        ],
    )(scalars, layer_id, w_key, w_value, gain_table)


def row_pairs(scalars_ref, source_ref, whole, shard, raw_ref):
    if not whole:
        return [(source_ref, raw_ref)]
    x = scalars_ref[1]
    pairs = []
    for i in range(raw_ref.shape[1] // shard):
        lanes = pl.ds(pl.multiple_of((2 * i + x) * shard, shard), shard)
        pairs.append((source_ref.at[:, lanes], raw_ref.at[:, pl.ds(i * shard, shard)]))
    return pairs


def multiply_kernel(shard, line, pieces, *refs):
    refs = list(refs)
    scalars_ref = refs.pop(0)
    sources = [[refs.pop(0) for _ in range(2 if i > 1 else 1)] for i in range(4)]
    key_ref, value_ref = refs.pop(0), refs.pop(0)
    mine = [[refs.pop(0) for _ in range(pieces)] for _ in range(line)]
    theirs = [None] + [[refs.pop(0) for _ in range(pieces)] for _ in range(line - 1)]
    scale_ref = refs.pop(0)
    key_keep, key_send, value_keep, value_send = refs[:4]
    weights, gains, parts, raw, sems = refs[4:]
    y, x, z, c = (scalars_ref[i] for i in range(4))
    half = shard // 2
    rows = half // pieces
    columns = key_ref.shape[1]
    width = 2 * columns
    pairs = []
    for d in range(line):
        for p in range(pieces):
            pairs.append((mine[d][p].at[pl.ds(rows, GAIN_ROWS), :], parts.at[d * pieces + p]))
        first = jnp.bitwise_xor(z, d) * shard
        if d == 0:
            for i, weight_ref in enumerate((key_ref, value_ref)):
                target = weights.at[
                    pl.ds(pl.multiple_of(first, shard), shard), pl.ds(i * columns, columns)
                ]
                pairs.append((weight_ref, target))
            continue
        for blocks, side in ((mine[d], y), (theirs[d], 1 - y)):
            for p, piece in enumerate(blocks):
                start = pl.multiple_of(first + side * half + p * rows, rows)
                pairs.append((piece.at[pl.ds(0, rows), :], weights.at[pl.ds(start, rows), :]))
    ends = [len(pairs)]
    for i, source in enumerate(sources):
        first = 0
        for chunk in source:
            target = raw.at[i, pl.ds(first, chunk.shape[0]), :]
            pairs += row_pairs(scalars_ref, chunk, i < 2, shard, target)
            first += chunk.shape[0]
        ends.append(len(pairs))
    copies = run_copies(pairs, sems)
    wait_all(copies[: ends[0]])
    for d in range(line):
        first = jnp.bitwise_xor(z, d) * shard
        for p in range(pieces):
            lanes = pl.ds(pl.multiple_of(first + p * width, width), width)
            gains[:, lanes] = parts[d * pieces + p]
    page = scale_ref.shape[1] // 2
    for i in range(4):
        if i % 2 == 0:
            wait_all(copies[ends[i] : ends[i + 2]])
            both = raw[i : i + 2].reshape(-1, raw.shape[2])
            products = jnp.dot(
                both * gains[0:1, :], weights[...], preferred_element_type=jnp.float32
            )
        product = products[(i % 2) * 2 * page : (i % 2 + 1) * 2 * page, :]
        source_x = jnp.bitwise_xor(x, i // 2)
        core = jnp.bitwise_xor(c, i % 2)
        for part in range(2):
            page_rows = slice(part * page, (part + 1) * page)
            scale = scale_ref[i, page_rows, :]
            for j in range(columns // HD):
                group = j * 4 + core * 2 + part
                owner = scalars_ref[4 + group]
                owner_z, owner_x = owner // 2, owner % 2
                results = [
                    product[page_rows, k * columns + j * HD : k * columns + (j + 1) * HD] * scale
                    for k in range(2)
                ]

                @pl.when(owner_x == x)
                def _():
                    key_keep[owner_z, source_x] = results[0]
                    value_keep[owner_z, source_x] = results[1]

                @pl.when(owner_x != x)
                def _():
                    key_send[owner_z, source_x] = results[0].astype(jnp.bfloat16)
                    value_send[owner_z, source_x] = results[1].astype(jnp.bfloat16)


def multiply(scalars, sources, w_key, w_value, mine, theirs, scale):
    shard, columns = w_key.shape
    line = len(mine)
    device_rows = scale.shape[1]
    pieces = len(mine[0])
    operands = [
        *[chunk for source in sources for chunk in source], w_key, w_value,
        *[piece for blocks in mine for piece in blocks],
        *[piece for blocks in theirs for piece in blocks],
    ]
    keep = jax.ShapeDtypeStruct((line, 2, device_rows // 2, HD), jnp.float32)
    send = jax.ShapeDtypeStruct((line, 2, device_rows // 2, HD), jnp.bfloat16)
    copies = line * pieces + 2 + 2 * (line - 1) * pieces + 2 * line + 4
    return pl.pallas_call(
        functools.partial(multiply_kernel, shard, line, pieces),
        in_specs=[SMEM] + [HBM] * len(operands) + [VMEM],
        out_specs=[VMEM] * 4,
        out_shape=[keep, send, keep, send],
        scratch_shapes=[
            pltpu.VMEM((line * shard, 2 * columns), jnp.bfloat16),
            pltpu.VMEM((GAIN_ROWS, line * shard), jnp.bfloat16),
            pltpu.VMEM((line * pieces, GAIN_ROWS, 2 * columns), jnp.bfloat16),
            pltpu.VMEM((4, device_rows, line * shard), jnp.bfloat16),
            pltpu.SemaphoreType.DMA((copies,)),
        ],
        compiler_params=pltpu.CompilerParams(vmem_limit_bytes=VMEM_LIMIT),
    )(scalars, *operands, scale)


def finish_key_kernel(scalars_ref, keep_ref, came_ref, cos_ref, sin_ref, *out_refs):
    x, z = scalars_ref[1], scalars_ref[2]
    page = keep_ref.shape[2]
    for d, out_ref in enumerate(out_refs):
        owner_z = jnp.bitwise_xor(z, d)
        owner = owner_z * 2 + x
        group = jnp.int32(0)
        for g in range(2 * len(out_refs)):
            group = jnp.where(scalars_ref[4 + g] == owner, g, group)
        page_class = group % 4
        for s in range(2):
            raw = keep_ref[owner_z, s] + came_ref[owner_z, s].astype(jnp.float32)
            raw = raw.astype(jnp.bfloat16).astype(jnp.float32)
            turned = pltpu.roll(raw, HD // 2, 1)
            rotated = raw * cos_ref[s * 4 + page_class] + turned * sin_ref[s * 4 + page_class]
            out_ref[s * page : (s + 1) * page, :] = rotated.astype(jnp.bfloat16)


def finish_value_kernel(scalars_ref, keep_ref, came_ref, *out_refs):
    z = scalars_ref[2]
    page = keep_ref.shape[2]
    for d, out_ref in enumerate(out_refs):
        owner_z = jnp.bitwise_xor(z, d)
        for s in range(2):
            raw = keep_ref[owner_z, s] + came_ref[owner_z, s].astype(jnp.float32)
            out_ref[s * page : (s + 1) * page, :] = raw.astype(jnp.bfloat16)


def finish(kernel, scalars, keep, came, *tables):
    vmem = pl.BlockSpec(memory_space=pltpu.VMEM)
    line, _, page, _ = keep.shape
    return pl.pallas_call(
        kernel,
        in_specs=[pl.BlockSpec(memory_space=pltpu.SMEM)] + [vmem] * (2 + len(tables)),
        out_specs=[vmem] * line,
        out_shape=[jax.ShapeDtypeStruct((2 * page, HD), jnp.bfloat16)] * line,
        compiler_params=pltpu.CompilerParams(vmem_limit_bytes=SMALL_VMEM_LIMIT),
    )(scalars, keep, came, *tables)


def place_kernel(scalars_ref, *refs):
    out_ref = refs[-1]
    z = scalars_ref[2]
    rows = refs[0].shape[0]
    for d, block_ref in enumerate(refs[:-1]):
        start = pl.multiple_of(jnp.bitwise_xor(z, d) * rows, rows)
        out_ref[pl.ds(start, rows), :] = block_ref[...]


def place(scalars, blocks):
    vmem = pl.BlockSpec(memory_space=pltpu.VMEM)
    return pl.pallas_call(
        place_kernel,
        in_specs=[pl.BlockSpec(memory_space=pltpu.SMEM)] + [vmem] * len(blocks),
        out_specs=vmem,
        out_shape=jax.ShapeDtypeStruct((len(blocks) * blocks[0].shape[0], HD), jnp.bfloat16),
    )(scalars, *blocks)


def after(value, *others):
    return lax.optimization_barrier((value, *others))[0]


def paired_shards(hidden, gain_table, layer_id, w_key, w_value, offsets, owner_map):
    tok_count = lax.axis_size("tok")
    line = tok_count // 2
    pieces = 2
    y, tok, c = lax.axis_index("group"), lax.axis_index("tok"), lax.axis_index("col")
    x, z = tok % 2, tok // 2
    shard = w_key.shape[0]
    device_rows = hidden.shape[0]
    page = device_rows // 2
    chunks = (page, device_rows - page)
    scalars = jnp.concatenate([jnp.stack([y, x, z, c]).astype(jnp.int32), owner_map])

    def over_x(values):
        return lax.ppermute(values, "tok", [(t, t ^ 1) for t in range(tok_count)])

    def over_z(values, distance):
        return lax.ppermute(values, "tok", [(t, t ^ (2 * distance)) for t in range(tok_count)])

    def over_y(values):
        return lax.ppermute(values, "group", [(0, 1), (1, 0)])

    def over_c(values):
        return lax.ppermute(values, "col", [(0, 1), (1, 0)])

    def squares(values):
        wide = values.astype(jnp.float32)
        return jnp.sum(wide * wide, axis=1)

    away = jnp.reshape(1 - x, (1,)).astype(jnp.int32)
    packed = pack_weights(scalars, layer_id, w_key, w_value, gain_table, pieces)
    head, tail = feature_half(hidden, away, shard, chunks)
    own_head = over_x(head)
    other = over_c(hidden)
    far = [over_z(piece, 2) for piece in packed]
    near = [over_z(packed[0], 1), over_z(after(packed[1], other), 1)]

    facts = jnp.stack(
        [
            jnp.concatenate([squares(hidden), squares(other)]),
            jnp.broadcast_to(offsets[0].astype(jnp.float32), (2 * device_rows,)),
        ]
    )
    near_y_0 = over_y(near[0])
    corner_0 = over_z(after(far[0], near[0], facts), 1)
    far_y_0 = over_y(after(far[0], near[0]))
    near_y_1 = over_y(after(near[1], far[0]))
    corner_1 = over_z(after(far[1], near[1], near_y_0), 1)
    far_y_1 = over_y(after(far[1], near[1], own_head))
    corner_y_0 = over_y(after(corner_0, near_y_1, far_y_0))
    pair_facts = over_x(facts)
    corner_y_1 = over_y(after(corner_1, far_y_1, pair_facts))
    near_y, far_y = [near_y_0, near_y_1], [far_y_0, far_y_1]
    corner, corner_y = [corner_0, corner_1], [corner_y_0, corner_y_1]
    own_tail = over_x(after(tail, near[0]))
    totals = jnp.concatenate([facts[0], pair_facts[0]])
    scale = lax.rsqrt(totals / hidden.shape[1] + 1e-05).reshape(4, device_rows, 1)
    scale = jnp.broadcast_to(scale, (4, device_rows, HD))
    starts = jnp.stack([facts[1, 0], pair_facts[1, 0]]).astype(jnp.int32)
    starts = jnp.where(x == 0, starts, starts[::-1])
    block = jnp.arange(2 * device_rows, dtype=jnp.int32)
    cosine, sine = rotary_table((starts[:, None] + block[None, :]).reshape(-1), HD)
    cosine = jnp.concatenate([cosine, cosine], axis=1).reshape(8, page, HD)
    sine = jnp.concatenate([-sine, sine], axis=1).reshape(8, page, HD)

    other_head = over_c(after(own_head, *corner_y))
    other_tail = over_c(after(own_tail, *corner_y))

    key_keep, key_send, value_keep, value_send = multiply(
        scalars, [[hidden], [other], [own_head, own_tail], [other_head, other_tail]], w_key, w_value,
        [packed, near, far, corner], [near_y, far_y, corner_y], scale,
    )
    key_came = over_x(key_send)
    value_came = over_x(after(value_send, key_came))
    keys = finish(finish_key_kernel, scalars, key_keep, key_came, cosine, sine)
    values = finish(finish_value_kernel, scalars, value_keep, value_came)
    outs = []
    for blocks in (keys, values):
        blocks = [blocks[0]] + [over_z(blocks[d], d) for d in range(1, line)]
        outs.append(place(scalars, blocks)[None])
    return tuple(outs)


def solution(mesh):
    in_specs = (
        P(("group", "tok", "col"), None),
        P(None, "tok"),
        P("group"),
        P("tok", "col"),
        P("tok", "col"),
        P(("group", "tok")),
        P("group"),
    )
    out_specs = (P("col", ("group", "tok"), None), P("col", ("group", "tok"), None))
    paired = mesh.shape["group"] == 2 and mesh.shape["tok"] == 8 and mesh.shape["col"] == 2
    shards = paired_shards if paired else general_shards
    return jax.shard_map(shards, mesh=mesh, in_specs=in_specs, out_specs=out_specs, check_vma=False)
```

```python
import functools
import math

import jax
import jax.numpy as jnp
from jax import lax
from jax.experimental import pallas as pl
from jax.experimental.pallas import tpu as pltpu
from jax.sharding import PartitionSpec as P

HD = 128
GAIN_ROWS = 16
VMEM_LIMIT = 58 * 2**20
SMALL_VMEM_LIMIT = 8 * 2**20


def rotary_table(position, size_head):
    half_size = size_head // 2
    frequency = jnp.power(
        jnp.float32(500000.0), -2.0 * jnp.arange(half_size, dtype=jnp.float32) / size_head
    )
    angle = jnp.mod(position.astype(jnp.float32)[:, None] * frequency[None, :], 2.0 * math.pi)
    return jnp.cos(angle), jnp.sin(angle)


def rotate(unrotated, position):
    half_size = unrotated.shape[-1] // 2
    cosine, sine = rotary_table(position, unrotated.shape[-1])
    cosine, sine = cosine[:, None, :], sine[:, None, :]
    values = unrotated.astype(jnp.float32)
    first = values[..., :half_size]
    second = values[..., half_size:]
    return jnp.concatenate(
        [first * cosine - second * sine, second * cosine + first * sine], axis=-1
    ).astype(jnp.bfloat16)


def normalize(values, squares_total, gain, feature_count):
    scale = lax.rsqrt(squares_total / feature_count + 1e-05)
    return (values.astype(jnp.float32) * scale[:, None] * gain.astype(jnp.float32)[None, :]).astype(
        jnp.bfloat16
    )


def general_shards(hidden, gain_table, layer_id, w_key, w_value, offsets, owner_map):
    tok_count = lax.axis_size("tok")
    col_count = lax.axis_size("col")
    gain_piece = lax.dynamic_index_in_dim(gain_table, layer_id[0], 0, keepdims=False)
    gain_full = lax.all_gather(gain_piece, "tok", axis=0, tiled=True)
    feature_count = gain_full.shape[0]
    block_rows = hidden.shape[0] * col_count
    tok_rows = lax.all_gather(hidden, "col", axis=0, tiled=True)
    wide = tok_rows.astype(jnp.float32)
    normed = normalize(tok_rows, jnp.sum(wide * wide, axis=1), gain_full, feature_count)
    key_raw, value_new = (
        jnp.dot(
            normed,
            lax.all_gather(weight, "tok", axis=0, tiled=True),
            preferred_element_type=jnp.float32,
        ).astype(jnp.bfloat16)
        for weight in (w_key, w_value)
    )
    heads_here = key_raw.shape[1] // HD
    classes = tok_count // heads_here
    page = block_rows // classes
    group_ids = jnp.arange(tok_count, dtype=jnp.int32)
    inverse = jnp.zeros((tok_count,), jnp.int32).at[owner_map].set(group_ids)

    def arrange_pages(values):
        grouped = (
            values.reshape(classes, page, heads_here, HD)
            .transpose(2, 0, 1, 3)
            .reshape(tok_count, page, HD)
        )
        return jnp.take(grouped, inverse, axis=0).reshape(tok_count * page, HD)

    position = offsets[0] + jnp.arange(block_rows, dtype=jnp.int32)
    key_new = rotate(key_raw.reshape(block_rows, heads_here, HD), position).reshape(block_rows, -1)
    key_out, value_out = (
        lax.all_to_all(arrange_pages(values), "tok", split_axis=0, concat_axis=0, tiled=True)
        for values in (key_new, value_new)
    )
    return (key_out.reshape(1, -1, HD), value_out.reshape(1, -1, HD))


def run_copies(pairs, sems):
    copies = [
        pltpu.make_async_copy(source, target, sems.at[i])
        for i, (source, target) in enumerate(pairs)
    ]
    for copy in copies:
        copy.start()
    return copies


def wait_all(copies):
    for copy in copies:
        copy.wait()


SMEM = pl.BlockSpec(memory_space=pltpu.SMEM)
VMEM = pl.BlockSpec(memory_space=pltpu.VMEM)
HBM = pl.BlockSpec(memory_space=pltpu.HBM)


def here():
    tok = lax.axis_index("tok")
    return lax.axis_index("group"), tok % 2, tok // 2, lax.axis_index("col")


def half_kernel(shard, hidden_ref, half_ref, sems):
    x = here()[1]
    pairs = []
    for i in range(half_ref.shape[1] // shard):
        lanes = pl.ds(pl.multiple_of((2 * i + 1 - x) * shard, shard), shard)
        pairs.append((hidden_ref.at[:, lanes], half_ref.at[:, pl.ds(i * shard, shard)]))
    wait_all(run_copies(pairs, sems))


def away_half(hidden, shard):
    rows, features = hidden.shape
    return pl.pallas_call(
        functools.partial(half_kernel, shard),
        in_specs=[HBM],
        out_specs=VMEM,
        out_shape=jax.ShapeDtypeStruct((rows, features // 2), hidden.dtype),
        scratch_shapes=[pltpu.SemaphoreType.DMA((features // shard // 2,))],
        compiler_params=pltpu.CompilerParams(vmem_limit_bytes=SMALL_VMEM_LIMIT),
    )(hidden)


def pack_kernel(layer_ref, key_ref, value_ref, gain_ref, *refs):
    *packed_refs, table, sems = refs
    shard, columns = key_ref.shape
    half = shard // 2
    width = 2 * columns
    gain_parts = shard // width
    layer = layer_ref[0]
    block = pl.multiple_of(layer // GAIN_ROWS * GAIN_ROWS, GAIN_ROWS)
    pairs = [(gain_ref.at[pl.ds(block, GAIN_ROWS), :], table)]
    for i, packed_ref in enumerate(packed_refs):
        count = PACKED[i][1]
        rows = half // count
        first = pl.multiple_of(here()[0] * half + PACKED[i][0] * rows, rows)
        for k, weight_ref in enumerate((key_ref, value_ref)):
            target = packed_ref.at[pl.ds(0, rows), pl.ds(k * columns, columns)]
            pairs.append((weight_ref.at[pl.ds(first, rows), :], target))
    copies = run_copies(pairs, sems)
    copies[0].wait()
    found = table[...].astype(jnp.float32)
    pick = lax.broadcasted_iota(jnp.int32, found.shape, 0) == layer % GAIN_ROWS
    gain = jnp.sum(jnp.where(pick, found, 0.0), axis=0, keepdims=True)
    for i, packed_ref in enumerate(packed_refs):
        index, count = PACKED[i]
        rows = half // count
        for p in range(gain_parts // count):
            part = index * (gain_parts // count) + p
            packed_ref[rows + p * GAIN_ROWS : rows + (p + 1) * GAIN_ROWS, :] = jnp.broadcast_to(
                gain[:, part * width : (part + 1) * width], (GAIN_ROWS, width)
            ).astype(packed_ref.dtype)
    wait_all(copies[1:])


PACKED = ((0, 2), (1, 2), (0, 1))


def pack_weights(layer_id, w_key, w_value, gain_table):
    shard, columns = w_key.shape
    rows = shard // 2 + shard // (2 * columns) * GAIN_ROWS
    return pl.pallas_call(
        pack_kernel,
        in_specs=[SMEM, HBM, HBM, HBM],
        out_specs=[VMEM] * len(PACKED),
        out_shape=[
            jax.ShapeDtypeStruct((rows // count, 2 * columns), w_key.dtype) for _, count in PACKED
        ],
        scratch_shapes=[
            pltpu.VMEM((GAIN_ROWS, gain_table.shape[1]), gain_table.dtype),
            pltpu.SemaphoreType.DMA((1 + 2 * len(PACKED),)),
        ],
        compiler_params=pltpu.CompilerParams(vmem_limit_bytes=SMALL_VMEM_LIMIT),
    )(layer_id, w_key, w_value, gain_table)


def group_of(owner_ref, owner):
    group = jnp.int32(0)
    for g in range(owner_ref.shape[0]):
        group = jnp.where(owner_ref[g] == owner, g, group)
    return group // 4, group % 4 // 2, group % 2


def multiply_kernel(shard, counts, which, *refs):
    refs = list(refs)
    owner_ref = refs.pop(0)
    sources = [refs.pop(0) for _ in range(4)]
    weight_ref = refs.pop(0)
    line = len(counts)
    mine = [[refs.pop(0) for _ in range(count)] for count in counts]
    theirs = [[]] + [[refs.pop(0) for _ in range(count)] for count in counts[1:]]
    keep, send, weights, gains, raw, total, sems = refs
    y, x, z, c = here()
    half = shard // 2
    columns = weight_ref.shape[1]
    width = 2 * columns
    _, _, page, _ = keep.shape
    device_rows = 2 * page
    pairs, ends = [], []
    for d in range(line):
        first = d * shard
        rows = half // counts[d]
        gain_parts = shard // width // counts[d]
        for i, packed in enumerate(mine[d]):
            for p in range(gain_parts):
                lanes = pl.ds(first + (i * gain_parts + p) * width, width)
                gain_rows = pl.ds(rows + p * GAIN_ROWS, GAIN_ROWS)
                pairs.append((packed.at[gain_rows, :], gains.at[:, lanes]))
        if d == 0:
            pairs.append((weight_ref, weights.at[pl.ds(first, shard), :]))
        picked = pl.ds(which * columns, columns)
        for blocks, side in ((mine[d] if d > 0 else [], y), (theirs[d], 1 - y)):
            for i, packed in enumerate(blocks):
                start = pl.multiple_of(first + side * half + i * rows, rows)
                target = weights.at[pl.ds(start, rows), :]
                pairs.append((packed.at[pl.ds(0, rows), picked], target))
        place_z = jnp.bitwise_xor(z, d)
        for i, source in enumerate(sources):
            block = 2 * place_z + x if i < 2 else place_z
            lanes = pl.ds(pl.multiple_of(block * shard, shard), shard)
            target = raw.at[pl.ds(i * device_rows, device_rows), pl.ds(first, shard)]
            pairs.append((source.at[:, lanes], target))
        ends.append(len(pairs))
    copies = run_copies(pairs, sems)
    for d in range(line):
        wait_all(copies[(ends[d - 1] if d > 0 else 0) : ends[d]])
        block = slice(d * shard, (d + 1) * shard)
        for i in range(2):
            span = slice(i * 2 * device_rows, (i + 1) * 2 * device_rows)
            product = jnp.dot(
                raw[span, block] * gains[0:1, block],
                weights[block, :],
                preferred_element_type=jnp.float32,
            )
            total[span, :] = product if d == 0 else total[span, :] + product
    for owner_z in range(line):
        for owner_x, out in ((x, keep), (1 - x, send)):
            j, core, part = group_of(owner_ref, owner_z * 2 + owner_x)
            lanes = pl.ds(pl.multiple_of(j * HD, HD), HD)
            for side in range(2):
                source = 2 * side + jnp.bitwise_xor(core, c)
                start = pl.multiple_of(source * device_rows + part * page, page)
                out[owner_z, jnp.bitwise_xor(x, side)] = total[pl.ds(start, page), lanes].astype(
                    out.dtype
                )


def multiply(owner_map, sources, weight, which, mine, theirs):
    shard, columns = weight.shape
    line = len(mine)
    device_rows = sources[0].shape[0]
    operands = [
        *sources, weight,
        *[packed for blocks in mine + theirs for packed in blocks],
    ]
    shape = (line, 2, device_rows // 2, HD)
    counts = tuple(len(blocks) for blocks in mine)
    copies = line * (shard // (2 * columns)) + 1 + 2 * sum(counts) + 4 * line
    return pl.pallas_call(
        functools.partial(multiply_kernel, shard, counts, which),
        in_specs=[SMEM] + [HBM] * len(operands),
        out_specs=[VMEM] * 2,
        out_shape=[
            jax.ShapeDtypeStruct(shape, jnp.float32),
            jax.ShapeDtypeStruct(shape, jnp.bfloat16),
        ],
        scratch_shapes=[
            pltpu.VMEM((line * shard, columns), jnp.bfloat16),
            pltpu.VMEM((GAIN_ROWS, line * shard), jnp.bfloat16),
            pltpu.VMEM((4 * device_rows, line * shard), jnp.bfloat16),
            pltpu.VMEM((4 * device_rows, columns), jnp.float32),
            pltpu.SemaphoreType.DMA((copies,)),
        ],
        compiler_params=pltpu.CompilerParams(vmem_limit_bytes=VMEM_LIMIT),
    )(owner_map, *operands)


def finish_kernel(line, turn, owner_ref, keep_ref, came_ref, scale_ref, *refs):
    out_refs = refs[-line:]
    _, x, z, c = here()
    page = keep_ref.shape[2]
    for d, out_ref in enumerate(out_refs):
        owner_z = jnp.bitwise_xor(z, d)
        _, core, part = group_of(owner_ref, owner_z * 2 + x)
        for s in range(2):
            source = 2 * jnp.bitwise_xor(x, s) + jnp.bitwise_xor(core, c)
            scale = scale_ref[source, pl.ds(pl.multiple_of(part * page, page), page), :]
            result = (keep_ref[owner_z, s] + came_ref[owner_z, s].astype(jnp.float32)) * scale
            if turn:
                cos_ref, sin_ref = refs[:2]
                result = result.astype(jnp.bfloat16).astype(jnp.float32)
                page_class = s * 4 + core * 2 + part
                turned = pltpu.roll(result, HD // 2, 1)
                result = result * cos_ref[page_class] + turned * sin_ref[page_class]
            out_ref[s * page : (s + 1) * page, :] = result.astype(jnp.bfloat16)


def finish(owner_map, keep, came, scale, *tables):
    line, _, page, _ = keep.shape
    return pl.pallas_call(
        functools.partial(finish_kernel, line, len(tables) > 0),
        in_specs=[SMEM] + [VMEM] * (3 + len(tables)),
        out_specs=[VMEM] * line,
        out_shape=[jax.ShapeDtypeStruct((2 * page, HD), jnp.bfloat16)] * line,
        compiler_params=pltpu.CompilerParams(vmem_limit_bytes=SMALL_VMEM_LIMIT),
    )(owner_map, keep, came, scale, *tables)


def place_kernel(*refs):
    out_ref = refs[-1]
    z = here()[2]
    rows = refs[0].shape[0]
    for d, block_ref in enumerate(refs[:-1]):
        start = pl.multiple_of(jnp.bitwise_xor(z, d) * rows, rows)
        out_ref[pl.ds(start, rows), :] = block_ref[...]


def place(blocks):
    return pl.pallas_call(
        place_kernel,
        in_specs=[VMEM] * len(blocks),
        out_specs=VMEM,
        out_shape=jax.ShapeDtypeStruct((len(blocks) * blocks[0].shape[0], HD), jnp.bfloat16),
        compiler_params=pltpu.CompilerParams(vmem_limit_bytes=SMALL_VMEM_LIMIT),
    )(*blocks)


def after(value, *others):
    return lax.optimization_barrier((value, *others))[0]


def paired_shards(hidden, gain_table, layer_id, w_key, w_value, offsets, owner_map):
    tok_count = lax.axis_size("tok")
    line = tok_count // 2
    _, x, _, _ = here()
    shard = w_key.shape[0]
    device_rows = hidden.shape[0]
    page = device_rows // 2

    def over_x(values):
        return lax.ppermute(values, "tok", [(t, t ^ 1) for t in range(tok_count)])

    def over_z(values, distance):
        return lax.ppermute(values, "tok", [(t, t ^ (2 * distance)) for t in range(tok_count)])

    def over_y(values):
        return lax.ppermute(values, "group", [(0, 1), (1, 0)])

    def over_c(values):
        return lax.ppermute(values, "col", [(0, 1), (1, 0)])

    other = over_c(hidden)
    pair_offset = over_x(offsets)
    away = away_half(hidden, shard)
    own_away = over_x(after(away, pair_offset))
    *pieces, packed = pack_weights(layer_id, after(w_key, away), w_value, gain_table)
    near_0 = over_z(pieces[0], 1)
    far_0 = over_z(pieces[0], 2)
    near_1 = over_z(after(pieces[1], other), 1)
    far_1 = over_z(after(pieces[1], near_0), 2)
    near_y_0 = over_y(near_0)

    wide = after(hidden, packed).astype(jnp.float32)
    own_squares = jnp.sum(wide * wide, axis=1)
    starts = jnp.where(x == 0, jnp.stack([offsets, pair_offset]), jnp.stack([pair_offset, offsets]))
    position = (starts + jnp.arange(2 * device_rows, dtype=jnp.int32)[None, :]).reshape(-1)
    cosine, sine = rotary_table(position, HD)
    cosine = jnp.concatenate([cosine, cosine], axis=1).reshape(8, page, HD)
    sine = jnp.concatenate([-sine, sine], axis=1).reshape(8, page, HD)

    corner_0 = over_z(after(far_0, near_0, own_squares), 1)
    near_y_1 = over_y(near_1)
    far_y_0 = over_y(after(far_0, near_y_0))
    corner_1 = over_z(after(far_1, near_y_1), 1)
    far_y_1 = over_y(after(far_1, near_y_1))
    corner_y_0 = over_y(after(corner_0, far_y_0, corner_1, cosine, sine))
    corner_y_1 = over_y(after(corner_1, far_y_1))
    other_away = over_c(after(own_away, corner_y_0, far_y_1))

    pair_squares = jnp.stack([own_squares, over_x(own_squares)])
    squares = jnp.stack([pair_squares, over_c(pair_squares)], axis=1).reshape(4, device_rows)
    scale = lax.rsqrt(squares / hidden.shape[1] + 1e-05)
    scale = jnp.broadcast_to(scale[:, :, None], (4, device_rows, HD))

    sources = [hidden, other, own_away, other_away]
    mine = [[packed], [near_0, near_1], [far_0, far_1], [corner_0, corner_1]]
    theirs = [[near_y_0, near_y_1], [far_y_0, far_y_1], [corner_y_0, corner_y_1]]
    key_keep, key_send = multiply(owner_map, sources, w_key, 0, mine, theirs)
    key_came = over_x(key_send)
    value_keep, value_send = multiply(
        owner_map, sources, after(w_value, key_send), 1, mine, theirs
    )
    value_came = over_x(value_send)
    keys = finish(owner_map, key_keep, key_came, scale, cosine, sine)
    values = finish(owner_map, value_keep, after(value_came, keys[0]), scale)
    keys = [keys[0]] + [over_z(keys[d], d) for d in range(1, line)]
    values = [values[0], after(values[1], *keys[1:]), *values[2:]]
    values = [values[0]] + [over_z(values[d], d) for d in range(1, line)]
    return (place(keys)[None], place(values)[None])


def solution(mesh):
    in_specs = (
        P(("group", "tok", "col"), None),
        P(None, "tok"),
        P("group"),
        P("tok", "col"),
        P("tok", "col"),
        P(("group", "tok")),
        P("group"),
    )
    out_specs = (P("col", ("group", "tok"), None), P("col", ("group", "tok"), None))
    paired = mesh.shape["group"] == 2 and mesh.shape["tok"] == 8 and mesh.shape["col"] == 2
    shards = paired_shards if paired else general_shards
    return jax.shard_map(shards, mesh=mesh, in_specs=in_specs, out_specs=out_specs, check_vma=False)
```

```python
import functools
import math

import jax
import jax.numpy as jnp
from jax import lax
from jax.experimental import pallas as pl
from jax.experimental.pallas import tpu as pltpu
from jax.sharding import PartitionSpec as P

HD = 128
GAIN_ROWS = 16
VMEM_LIMIT = 61 * 2**20
SMALL_VMEM_LIMIT = 8 * 2**20


def rotary_table(position, size_head):
    half_size = size_head // 2
    frequency = jnp.power(
        jnp.float32(500000.0), -2.0 * jnp.arange(half_size, dtype=jnp.float32) / size_head
    )
    angle = jnp.mod(position.astype(jnp.float32)[:, None] * frequency[None, :], 2.0 * math.pi)
    return jnp.cos(angle), jnp.sin(angle)


def rotate(unrotated, position):
    half_size = unrotated.shape[-1] // 2
    cosine, sine = rotary_table(position, unrotated.shape[-1])
    cosine, sine = cosine[:, None, :], sine[:, None, :]
    values = unrotated.astype(jnp.float32)
    first = values[..., :half_size]
    second = values[..., half_size:]
    return jnp.concatenate(
        [first * cosine - second * sine, second * cosine + first * sine], axis=-1
    ).astype(jnp.bfloat16)


def normalize(values, squares_total, gain, feature_count):
    scale = lax.rsqrt(squares_total / feature_count + 1e-05)
    return (values.astype(jnp.float32) * scale[:, None] * gain.astype(jnp.float32)[None, :]).astype(
        jnp.bfloat16
    )


def general_shards(hidden, gain_table, layer_id, w_key, w_value, offsets, owner_map):
    tok_count = lax.axis_size("tok")
    col_count = lax.axis_size("col")
    gain_piece = lax.dynamic_index_in_dim(gain_table, layer_id[0], 0, keepdims=False)
    gain_full = lax.all_gather(gain_piece, "tok", axis=0, tiled=True)
    feature_count = gain_full.shape[0]
    block_rows = hidden.shape[0] * col_count
    tok_rows = lax.all_gather(hidden, "col", axis=0, tiled=True)
    wide = tok_rows.astype(jnp.float32)
    normed = normalize(tok_rows, jnp.sum(wide * wide, axis=1), gain_full, feature_count)
    key_raw, value_new = (
        jnp.dot(
            normed,
            lax.all_gather(weight, "tok", axis=0, tiled=True),
            preferred_element_type=jnp.float32,
        ).astype(jnp.bfloat16)
        for weight in (w_key, w_value)
    )
    heads_here = key_raw.shape[1] // HD
    classes = tok_count // heads_here
    page = block_rows // classes
    group_ids = jnp.arange(tok_count, dtype=jnp.int32)
    inverse = jnp.zeros((tok_count,), jnp.int32).at[owner_map].set(group_ids)

    def arrange_pages(values):
        grouped = (
            values.reshape(classes, page, heads_here, HD)
            .transpose(2, 0, 1, 3)
            .reshape(tok_count, page, HD)
        )
        return jnp.take(grouped, inverse, axis=0).reshape(tok_count * page, HD)

    position = offsets[0] + jnp.arange(block_rows, dtype=jnp.int32)
    key_new = rotate(key_raw.reshape(block_rows, heads_here, HD), position).reshape(block_rows, -1)
    key_out, value_out = (
        lax.all_to_all(arrange_pages(values), "tok", split_axis=0, concat_axis=0, tiled=True)
        for values in (key_new, value_new)
    )
    return (key_out.reshape(1, -1, HD), value_out.reshape(1, -1, HD))


def run_copies(pairs, sems):
    copies = [
        pltpu.make_async_copy(source, target, sems.at[i])
        for i, (source, target) in enumerate(pairs)
    ]
    for copy in copies:
        copy.start()
    return copies


def wait_all(copies):
    for copy in copies:
        copy.wait()


SMEM = pl.BlockSpec(memory_space=pltpu.SMEM)
VMEM = pl.BlockSpec(memory_space=pltpu.VMEM)
HBM = pl.BlockSpec(memory_space=pltpu.HBM)


def here():
    tok = lax.axis_index("tok")
    return lax.axis_index("group"), tok % 2, tok // 2, lax.axis_index("col")


def half_kernel(shard, hidden_ref, half_ref, sems):
    x = here()[1]
    pairs = []
    for i in range(half_ref.shape[1] // shard):
        lanes = pl.ds(pl.multiple_of((2 * i + 1 - x) * shard, shard), shard)
        pairs.append((hidden_ref.at[:, lanes], half_ref.at[:, pl.ds(i * shard, shard)]))
    wait_all(run_copies(pairs, sems))


def away_half(hidden, shard):
    rows, features = hidden.shape
    return pl.pallas_call(
        functools.partial(half_kernel, shard),
        in_specs=[HBM],
        out_specs=VMEM,
        out_shape=jax.ShapeDtypeStruct((rows, features // 2), hidden.dtype),
        scratch_shapes=[pltpu.SemaphoreType.DMA((features // shard // 2,))],
        compiler_params=pltpu.CompilerParams(vmem_limit_bytes=SMALL_VMEM_LIMIT),
    )(hidden)


def pack_kernel(layer_ref, key_ref, value_ref, gain_ref, *refs):
    *packed_refs, table, sems = refs
    shard, columns = key_ref.shape
    half = shard // 2
    width = 2 * columns
    gain_parts = shard // width
    layer = layer_ref[0]
    block = pl.multiple_of(layer // GAIN_ROWS * GAIN_ROWS, GAIN_ROWS)
    pairs = [(gain_ref.at[pl.ds(block, GAIN_ROWS), :], table)]
    for i, packed_ref in enumerate(packed_refs):
        count = PACKED[i][1]
        rows = half // count
        first = pl.multiple_of(here()[0] * half + PACKED[i][0] * rows, rows)
        for k, weight_ref in enumerate((key_ref, value_ref)):
            target = packed_ref.at[pl.ds(0, rows), pl.ds(k * columns, columns)]
            pairs.append((weight_ref.at[pl.ds(first, rows), :], target))
    copies = run_copies(pairs, sems)
    copies[0].wait()
    found = table[...].astype(jnp.float32)
    pick = lax.broadcasted_iota(jnp.int32, found.shape, 0) == layer % GAIN_ROWS
    gain = jnp.sum(jnp.where(pick, found, 0.0), axis=0, keepdims=True)
    for i, packed_ref in enumerate(packed_refs):
        index, count = PACKED[i]
        rows = half // count
        for p in range(gain_parts // count):
            part = index * (gain_parts // count) + p
            packed_ref[rows + p * GAIN_ROWS : rows + (p + 1) * GAIN_ROWS, :] = jnp.broadcast_to(
                gain[:, part * width : (part + 1) * width], (GAIN_ROWS, width)
            ).astype(packed_ref.dtype)
    wait_all(copies[1:])


PACKED = ((0, 2), (1, 2), (0, 1))


def pack_weights(layer_id, w_key, w_value, gain_table):
    shard, columns = w_key.shape
    rows = shard // 2 + shard // (2 * columns) * GAIN_ROWS
    return pl.pallas_call(
        pack_kernel,
        in_specs=[SMEM, HBM, HBM, HBM],
        out_specs=[VMEM] * len(PACKED),
        out_shape=[
            jax.ShapeDtypeStruct((rows // count, 2 * columns), w_key.dtype) for _, count in PACKED
        ],
        scratch_shapes=[
            pltpu.VMEM((GAIN_ROWS, gain_table.shape[1]), gain_table.dtype),
            pltpu.SemaphoreType.DMA((1 + 2 * len(PACKED),)),
        ],
        compiler_params=pltpu.CompilerParams(vmem_limit_bytes=SMALL_VMEM_LIMIT),
    )(layer_id, w_key, w_value, gain_table)


def group_of(owner_ref, owner):
    group = jnp.int32(0)
    for g in range(owner_ref.shape[0]):
        group = jnp.where(owner_ref[g] == owner, g, group)
    return group // 4, group % 4 // 2, group % 2


def multiply_kernel(shard, counts, which, *refs):
    refs = list(refs)
    owner_ref = refs.pop(0)
    sources = [refs.pop(0) for _ in range(4)]
    weight_ref = refs.pop(0)
    line = len(counts)
    mine = [[refs.pop(0) for _ in range(count)] for count in counts]
    theirs = [[]] + [[refs.pop(0) for _ in range(count)] for count in counts[1:]]
    keep, send, weights, gains, raw, total, sems = refs
    y, x, z, c = here()
    half = shard // 2
    columns = weight_ref.shape[1]
    width = 2 * columns
    _, _, page, _ = keep.shape
    device_rows = 2 * page
    pairs, ends = [], []
    for d in range(line):
        first = d * shard
        rows = half // counts[d]
        gain_parts = shard // width // counts[d]
        for i, packed in enumerate(mine[d]):
            for p in range(gain_parts):
                lanes = pl.ds(first + (i * gain_parts + p) * width, width)
                gain_rows = pl.ds(rows + p * GAIN_ROWS, GAIN_ROWS)
                pairs.append((packed.at[gain_rows, :], gains.at[:, lanes]))
        if d == 0:
            pairs.append((weight_ref, weights.at[pl.ds(first, shard), :]))
        picked = pl.ds(which * columns, columns)
        for blocks, side in ((mine[d] if d > 0 else [], y), (theirs[d], 1 - y)):
            for i, packed in enumerate(blocks):
                start = pl.multiple_of(first + side * half + i * rows, rows)
                target = weights.at[pl.ds(start, rows), :]
                pairs.append((packed.at[pl.ds(0, rows), picked], target))
        place_z = jnp.bitwise_xor(z, d)
        for i, source in enumerate(sources):
            block = 2 * place_z + x if i < 2 else place_z
            lanes = pl.ds(pl.multiple_of(block * shard, shard), shard)
            target = raw.at[pl.ds(i * device_rows, device_rows), pl.ds(first, shard)]
            pairs.append((source.at[:, lanes], target))
        ends.append(len(pairs))
    copies = run_copies(pairs, sems)
    for d in range(line):
        wait_all(copies[(ends[d - 1] if d > 0 else 0) : ends[d]])
        block = slice(d * shard, (d + 1) * shard)
        for i in range(2):
            span = slice(i * 2 * device_rows, (i + 1) * 2 * device_rows)
            product = jnp.dot(
                raw[span, block] * gains[0:1, block],
                weights[block, :],
                preferred_element_type=jnp.float32,
            )
            total[span, :] = product if d == 0 else total[span, :] + product
    for owner_z in range(line):
        for owner_x, out in ((x, keep), (1 - x, send)):
            j, core, part = group_of(owner_ref, owner_z * 2 + owner_x)
            lanes = pl.ds(pl.multiple_of(j * HD, HD), HD)
            for side in range(2):
                source = 2 * side + jnp.bitwise_xor(core, c)
                start = pl.multiple_of(source * device_rows + part * page, page)
                out[owner_z, jnp.bitwise_xor(x, side)] = total[pl.ds(start, page), lanes].astype(
                    out.dtype
                )


def multiply(owner_map, sources, weight, which, mine, theirs):
    shard, columns = weight.shape
    line = len(mine)
    device_rows = sources[0].shape[0]
    operands = [
        *sources, weight,
        *[packed for blocks in mine + theirs for packed in blocks],
    ]
    shape = (line, 2, device_rows // 2, HD)
    counts = tuple(len(blocks) for blocks in mine)
    copies = line * (shard // (2 * columns)) + 1 + 2 * sum(counts) + 4 * line
    return pl.pallas_call(
        functools.partial(multiply_kernel, shard, counts, which),
        in_specs=[SMEM] + [HBM] * len(operands),
        out_specs=[VMEM] * 2,
        out_shape=[
            jax.ShapeDtypeStruct(shape, jnp.float32),
            jax.ShapeDtypeStruct(shape, jnp.bfloat16),
        ],
        scratch_shapes=[
            pltpu.VMEM((line * shard, columns), jnp.bfloat16),
            pltpu.VMEM((GAIN_ROWS, line * shard), jnp.bfloat16),
            pltpu.VMEM((4 * device_rows, line * shard), jnp.bfloat16),
            pltpu.VMEM((4 * device_rows, columns), jnp.float32),
            pltpu.SemaphoreType.DMA((copies,)),
        ],
        compiler_params=pltpu.CompilerParams(vmem_limit_bytes=VMEM_LIMIT),
    )(owner_map, *operands)


def finish_kernel(line, turn, owner_ref, keep_ref, came_ref, scale_ref, *refs):
    out_refs = refs[-line:]
    _, x, z, c = here()
    page = keep_ref.shape[2]
    for d, out_ref in enumerate(out_refs):
        owner_z = jnp.bitwise_xor(z, d)
        _, core, part = group_of(owner_ref, owner_z * 2 + x)
        for s in range(2):
            source = 2 * jnp.bitwise_xor(x, s) + jnp.bitwise_xor(core, c)
            scale = scale_ref[source, pl.ds(pl.multiple_of(part * page, page), page), :]
            result = (keep_ref[owner_z, s] + came_ref[owner_z, s].astype(jnp.float32)) * scale
            if turn:
                cos_ref, sin_ref = refs[:2]
                result = result.astype(jnp.bfloat16).astype(jnp.float32)
                page_class = s * 4 + core * 2 + part
                turned = pltpu.roll(result, HD // 2, 1)
                result = result * cos_ref[page_class] + turned * sin_ref[page_class]
            out_ref[s * page : (s + 1) * page, :] = result.astype(jnp.bfloat16)


def finish(owner_map, keep, came, scale, *tables):
    line, _, page, _ = keep.shape
    return pl.pallas_call(
        functools.partial(finish_kernel, line, len(tables) > 0),
        in_specs=[SMEM] + [VMEM] * (3 + len(tables)),
        out_specs=[VMEM] * line,
        out_shape=[jax.ShapeDtypeStruct((2 * page, HD), jnp.bfloat16)] * line,
        compiler_params=pltpu.CompilerParams(vmem_limit_bytes=SMALL_VMEM_LIMIT),
    )(owner_map, keep, came, scale, *tables)


def place_kernel(*refs):
    out_ref = refs[-1]
    z = here()[2]
    rows = refs[0].shape[0]
    for d, block_ref in enumerate(refs[:-1]):
        start = pl.multiple_of(jnp.bitwise_xor(z, d) * rows, rows)
        out_ref[pl.ds(start, rows), :] = block_ref[...]


def place(blocks):
    return pl.pallas_call(
        place_kernel,
        in_specs=[VMEM] * len(blocks),
        out_specs=VMEM,
        out_shape=jax.ShapeDtypeStruct((len(blocks) * blocks[0].shape[0], HD), jnp.bfloat16),
        compiler_params=pltpu.CompilerParams(vmem_limit_bytes=SMALL_VMEM_LIMIT),
    )(*blocks)


def after(value, *others):
    return lax.optimization_barrier((value, *others))[0]


def paired_shards(hidden, gain_table, layer_id, w_key, w_value, offsets, owner_map):
    tok_count = lax.axis_size("tok")
    line = tok_count // 2
    _, x, _, _ = here()
    shard = w_key.shape[0]
    device_rows = hidden.shape[0]
    page = device_rows // 2

    def over_x(values):
        return lax.ppermute(values, "tok", [(t, t ^ 1) for t in range(tok_count)])

    def over_z(values, distance):
        return lax.ppermute(values, "tok", [(t, t ^ (2 * distance)) for t in range(tok_count)])

    def over_y(values):
        return lax.ppermute(values, "group", [(0, 1), (1, 0)])

    def over_c(values):
        return lax.ppermute(values, "col", [(0, 1), (1, 0)])

    other = over_c(hidden)
    away = away_half(hidden, shard)
    own_away = over_x(away)
    *pieces, packed = pack_weights(layer_id, after(w_key, away), w_value, gain_table)
    near_0 = over_z(pieces[0], 1)
    far_0 = over_z(pieces[0], 2)
    near_1 = over_z(after(pieces[1], other), 1)
    far_1 = over_z(after(pieces[1], near_0), 2)
    near_y_0 = over_y(near_0)

    wide = after(hidden, packed).astype(jnp.float32)
    own_squares = jnp.sum(wide * wide, axis=1)
    corner_0 = over_z(after(far_0, near_0, own_squares), 1)
    near_y_1 = over_y(near_1)
    far_y_0 = over_y(after(far_0, near_y_0))
    corner_1 = over_z(after(far_1, near_y_1), 1)
    far_y_1 = over_y(after(far_1, near_y_1))
    corner_y_0 = over_y(after(corner_0, far_y_0, corner_1))
    corner_y_1 = over_y(after(corner_1, far_y_1))
    start = jnp.broadcast_to(offsets[0].astype(jnp.float32), (device_rows,))
    own_facts = jnp.stack([own_squares, start])
    came_facts = over_x(after(own_facts, own_away))
    pair_facts = jnp.stack([own_facts, came_facts])
    other_away = over_c(after(own_away, corner_y_0, far_y_1, came_facts))

    starts = jnp.where(x == 0, pair_facts[:, 1, 0], pair_facts[::-1, 1, 0]).astype(jnp.int32)
    position = (starts[:, None] + jnp.arange(2 * device_rows, dtype=jnp.int32)).reshape(-1)
    cosine, sine = rotary_table(position, HD)
    cosine = jnp.concatenate([cosine, cosine], axis=1).reshape(8, page, HD)
    sine = jnp.concatenate([-sine, sine], axis=1).reshape(8, page, HD)
    pair_squares = pair_facts[:, 0]
    squares = jnp.stack([pair_squares, over_c(after(pair_squares, corner_y_1))], axis=1).reshape(4, device_rows)
    scale = lax.rsqrt(squares / hidden.shape[1] + 1e-05)
    scale = jnp.broadcast_to(scale[:, :, None], (4, device_rows, HD))

    sources = [hidden, other, own_away, other_away]
    mine = [[packed], [near_0, near_1], [far_0, far_1], [corner_0, corner_1]]
    theirs = [[near_y_0, near_y_1], [far_y_0, far_y_1], [corner_y_0, corner_y_1]]
    key_keep, key_send = multiply(
        owner_map, sources, after(w_key, scale, cosine, sine), 0, mine, theirs
    )
    key_came = over_x(key_send)
    value_keep, value_send = multiply(
        owner_map, sources, after(w_value, key_send), 1, mine, theirs
    )
    value_came = over_x(value_send)
    keys = finish(owner_map, key_keep, key_came, scale, cosine, sine)
    values = finish(owner_map, value_keep, after(value_came, keys[0]), scale)
    keys = [keys[0]] + [over_z(keys[d], d) for d in range(1, line)]
    values = [values[0], after(values[1], *keys[1:]), *values[2:]]
    values = [values[0]] + [over_z(values[d], d) for d in range(1, line)]
    return (place(keys)[None], place(values)[None])


def solution(mesh):
    in_specs = (
        P(("group", "tok", "col"), None),
        P(None, "tok"),
        P("group"),
        P("tok", "col"),
        P("tok", "col"),
        P(("group", "tok")),
        P("group"),
    )
    out_specs = (P("col", ("group", "tok"), None), P("col", ("group", "tok"), None))
    paired = mesh.shape["group"] == 2 and mesh.shape["tok"] == 8 and mesh.shape["col"] == 2
    shards = paired_shards if paired else general_shards
    return jax.shard_map(shards, mesh=mesh, in_specs=in_specs, out_specs=out_specs, check_vma=False)
```

```python
import functools
import math

import jax
import jax.numpy as jnp
from jax import lax
from jax.experimental import pallas as pl
from jax.experimental.pallas import tpu as pltpu
from jax.sharding import PartitionSpec as P

HD = 128
GAIN_ROWS = 16
VMEM_LIMIT = 61 * 2**20
SMALL_VMEM_LIMIT = 8 * 2**20


def rotary_table(position, size_head):
    half_size = size_head // 2
    frequency = jnp.power(
        jnp.float32(500000.0), -2.0 * jnp.arange(half_size, dtype=jnp.float32) / size_head
    )
    angle = jnp.mod(position.astype(jnp.float32)[:, None] * frequency[None, :], 2.0 * math.pi)
    return jnp.cos(angle), jnp.sin(angle)


def rotate(unrotated, position):
    half_size = unrotated.shape[-1] // 2
    cosine, sine = rotary_table(position, unrotated.shape[-1])
    cosine, sine = cosine[:, None, :], sine[:, None, :]
    values = unrotated.astype(jnp.float32)
    first = values[..., :half_size]
    second = values[..., half_size:]
    return jnp.concatenate(
        [first * cosine - second * sine, second * cosine + first * sine], axis=-1
    ).astype(jnp.bfloat16)


def normalize(values, squares_total, gain, feature_count):
    scale = lax.rsqrt(squares_total / feature_count + 1e-05)
    return (values.astype(jnp.float32) * scale[:, None] * gain.astype(jnp.float32)[None, :]).astype(
        jnp.bfloat16
    )


def general_shards(hidden, gain_table, layer_id, w_key, w_value, offsets, owner_map):
    tok_count = lax.axis_size("tok")
    col_count = lax.axis_size("col")
    gain_piece = lax.dynamic_index_in_dim(gain_table, layer_id[0], 0, keepdims=False)
    gain_full = lax.all_gather(gain_piece, "tok", axis=0, tiled=True)
    feature_count = gain_full.shape[0]
    block_rows = hidden.shape[0] * col_count
    tok_rows = lax.all_gather(hidden, "col", axis=0, tiled=True)
    wide = tok_rows.astype(jnp.float32)
    normed = normalize(tok_rows, jnp.sum(wide * wide, axis=1), gain_full, feature_count)
    key_raw, value_new = (
        jnp.dot(
            normed,
            lax.all_gather(weight, "tok", axis=0, tiled=True),
            preferred_element_type=jnp.float32,
        ).astype(jnp.bfloat16)
        for weight in (w_key, w_value)
    )
    heads_here = key_raw.shape[1] // HD
    classes = tok_count // heads_here
    page = block_rows // classes
    group_ids = jnp.arange(tok_count, dtype=jnp.int32)
    inverse = jnp.zeros((tok_count,), jnp.int32).at[owner_map].set(group_ids)

    def arrange_pages(values):
        grouped = (
            values.reshape(classes, page, heads_here, HD)
            .transpose(2, 0, 1, 3)
            .reshape(tok_count, page, HD)
        )
        return jnp.take(grouped, inverse, axis=0).reshape(tok_count * page, HD)

    position = offsets[0] + jnp.arange(block_rows, dtype=jnp.int32)
    key_new = rotate(key_raw.reshape(block_rows, heads_here, HD), position).reshape(block_rows, -1)
    key_out, value_out = (
        lax.all_to_all(arrange_pages(values), "tok", split_axis=0, concat_axis=0, tiled=True)
        for values in (key_new, value_new)
    )
    return (key_out.reshape(1, -1, HD), value_out.reshape(1, -1, HD))


def run_copies(pairs, sems):
    copies = [
        pltpu.make_async_copy(source, target, sems.at[i])
        for i, (source, target) in enumerate(pairs)
    ]
    for copy in copies:
        copy.start()
    return copies


def wait_all(copies):
    for copy in copies:
        copy.wait()


SMEM = pl.BlockSpec(memory_space=pltpu.SMEM)
VMEM = pl.BlockSpec(memory_space=pltpu.VMEM)
HBM = pl.BlockSpec(memory_space=pltpu.HBM)


def here():
    tok = lax.axis_index("tok")
    return lax.axis_index("group"), tok % 2, tok // 2, lax.axis_index("col")


def half_kernel(shard, hidden_ref, half_ref, sems):
    x = here()[1]
    pairs = []
    for i in range(half_ref.shape[1] // shard):
        lanes = pl.ds(pl.multiple_of((2 * i + 1 - x) * shard, shard), shard)
        pairs.append((hidden_ref.at[:, lanes], half_ref.at[:, pl.ds(i * shard, shard)]))
    wait_all(run_copies(pairs, sems))


def away_half(hidden, shard):
    rows, features = hidden.shape
    return pl.pallas_call(
        functools.partial(half_kernel, shard),
        in_specs=[HBM],
        out_specs=VMEM,
        out_shape=jax.ShapeDtypeStruct((rows, features // 2), hidden.dtype),
        scratch_shapes=[pltpu.SemaphoreType.DMA((features // shard // 2,))],
        compiler_params=pltpu.CompilerParams(vmem_limit_bytes=SMALL_VMEM_LIMIT),
    )(hidden)


def pack_kernel(layer_ref, key_ref, value_ref, gain_ref, *refs):
    *packed_refs, table, sems = refs
    shard, columns = key_ref.shape
    half = shard // 2
    width = 2 * columns
    gain_parts = shard // width
    layer = layer_ref[0]
    block = pl.multiple_of(layer // GAIN_ROWS * GAIN_ROWS, GAIN_ROWS)
    pairs = [(gain_ref.at[pl.ds(block, GAIN_ROWS), :], table)]
    for i, packed_ref in enumerate(packed_refs):
        count = PACKED[i][1]
        rows = half // count
        first = pl.multiple_of(here()[0] * half + PACKED[i][0] * rows, rows)
        for k, weight_ref in enumerate((key_ref, value_ref)):
            target = packed_ref.at[pl.ds(0, rows), pl.ds(k * columns, columns)]
            pairs.append((weight_ref.at[pl.ds(first, rows), :], target))
    copies = run_copies(pairs, sems)
    copies[0].wait()
    found = table[...].astype(jnp.float32)
    pick = lax.broadcasted_iota(jnp.int32, found.shape, 0) == layer % GAIN_ROWS
    gain = jnp.sum(jnp.where(pick, found, 0.0), axis=0, keepdims=True)
    for i, packed_ref in enumerate(packed_refs):
        index, count = PACKED[i]
        rows = half // count
        for p in range(gain_parts // count):
            part = index * (gain_parts // count) + p
            packed_ref[rows + p * GAIN_ROWS : rows + (p + 1) * GAIN_ROWS, :] = jnp.broadcast_to(
                gain[:, part * width : (part + 1) * width], (GAIN_ROWS, width)
            ).astype(packed_ref.dtype)
    wait_all(copies[1:])


PACKED = ((0, 2), (1, 2), (0, 1))


def pack_weights(layer_id, w_key, w_value, gain_table):
    shard, columns = w_key.shape
    rows = shard // 2 + shard // (2 * columns) * GAIN_ROWS
    return pl.pallas_call(
        pack_kernel,
        in_specs=[SMEM, HBM, HBM, HBM],
        out_specs=[VMEM] * len(PACKED),
        out_shape=[
            jax.ShapeDtypeStruct((rows // count, 2 * columns), w_key.dtype) for _, count in PACKED
        ],
        scratch_shapes=[
            pltpu.VMEM((GAIN_ROWS, gain_table.shape[1]), gain_table.dtype),
            pltpu.SemaphoreType.DMA((1 + 2 * len(PACKED),)),
        ],
        compiler_params=pltpu.CompilerParams(vmem_limit_bytes=SMALL_VMEM_LIMIT),
    )(layer_id, w_key, w_value, gain_table)


def group_of(owner_ref, owner):
    group = jnp.int32(0)
    for g in range(owner_ref.shape[0]):
        group = jnp.where(owner_ref[g] == owner, g, group)
    return group // 4, group % 4 // 2, group % 2


def multiply_kernel(shard, counts, which, *refs):
    refs = list(refs)
    owner_ref = refs.pop(0)
    sources = [refs.pop(0) for _ in range(4)]
    weight_ref = refs.pop(0)
    line = len(counts)
    mine = [[refs.pop(0) for _ in range(count)] for count in counts]
    theirs = [[]] + [[refs.pop(0) for _ in range(count)] for count in counts[1:]]
    keep, send, weights, gains, raw, total, sems = refs
    y, x, z, c = here()
    half = shard // 2
    columns = weight_ref.shape[1]
    width = 2 * columns
    _, _, page, _ = keep.shape
    device_rows = 2 * page
    pairs, ends = [], []
    for d in range(line):
        first = d * shard
        rows = half // counts[d]
        gain_parts = shard // width // counts[d]
        for i, packed in enumerate(mine[d]):
            for p in range(gain_parts):
                lanes = pl.ds(first + (i * gain_parts + p) * width, width)
                gain_rows = pl.ds(rows + p * GAIN_ROWS, GAIN_ROWS)
                pairs.append((packed.at[gain_rows, :], gains.at[:, lanes]))
        if d == 0:
            pairs.append((weight_ref, weights.at[pl.ds(first, shard), :]))
        picked = pl.ds(which * columns, columns)
        for blocks, side in ((mine[d] if d > 0 else [], y), (theirs[d], 1 - y)):
            for i, packed in enumerate(blocks):
                start = pl.multiple_of(first + side * half + i * rows, rows)
                target = weights.at[pl.ds(start, rows), :]
                pairs.append((packed.at[pl.ds(0, rows), picked], target))
        place_z = jnp.bitwise_xor(z, d)
        for i, source in enumerate(sources):
            block = 2 * place_z + x if i < 2 else place_z
            lanes = pl.ds(pl.multiple_of(block * shard, shard), shard)
            target = raw.at[pl.ds(i * device_rows, device_rows), pl.ds(first, shard)]
            pairs.append((source.at[:, lanes], target))
        ends.append(len(pairs))
    copies = run_copies(pairs, sems)
    for d in range(line):
        wait_all(copies[(ends[d - 1] if d > 0 else 0) : ends[d]])
        block = slice(d * shard, (d + 1) * shard)
        for i in range(2):
            span = slice(i * 2 * device_rows, (i + 1) * 2 * device_rows)
            product = jnp.dot(
                raw[span, block] * gains[0:1, block],
                weights[block, :],
                preferred_element_type=jnp.float32,
            )
            total[span, :] = product if d == 0 else total[span, :] + product
    for owner_z in range(line):
        for owner_x, out in ((x, keep), (1 - x, send)):
            j, core, part = group_of(owner_ref, owner_z * 2 + owner_x)
            lanes = pl.ds(pl.multiple_of(j * HD, HD), HD)
            for side in range(2):
                source = 2 * side + jnp.bitwise_xor(core, c)
                start = pl.multiple_of(source * device_rows + part * page, page)
                out[owner_z, jnp.bitwise_xor(x, side)] = total[pl.ds(start, page), lanes].astype(
                    out.dtype
                )


def multiply(owner_map, sources, weight, which, mine, theirs):
    shard, columns = weight.shape
    line = len(mine)
    device_rows = sources[0].shape[0]
    operands = [
        *sources, weight,
        *[packed for blocks in mine + theirs for packed in blocks],
    ]
    shape = (line, 2, device_rows // 2, HD)
    counts = tuple(len(blocks) for blocks in mine)
    copies = line * (shard // (2 * columns)) + 1 + 2 * sum(counts) + 4 * line
    return pl.pallas_call(
        functools.partial(multiply_kernel, shard, counts, which),
        in_specs=[SMEM] + [HBM] * len(operands),
        out_specs=[VMEM] * 2,
        out_shape=[
            jax.ShapeDtypeStruct(shape, jnp.float32),
            jax.ShapeDtypeStruct(shape, jnp.bfloat16),
        ],
        scratch_shapes=[
            pltpu.VMEM((line * shard, columns), jnp.bfloat16),
            pltpu.VMEM((GAIN_ROWS, line * shard), jnp.bfloat16),
            pltpu.VMEM((4 * device_rows, line * shard), jnp.bfloat16),
            pltpu.VMEM((4 * device_rows, columns), jnp.float32),
            pltpu.SemaphoreType.DMA((copies,)),
        ],
        compiler_params=pltpu.CompilerParams(vmem_limit_bytes=VMEM_LIMIT),
    )(owner_map, *operands)


def finish_kernel(line, turn, owner_ref, keep_ref, came_ref, scale_ref, *refs):
    out_refs = refs[-line:]
    _, x, z, c = here()
    page = keep_ref.shape[2]
    for d, out_ref in enumerate(out_refs):
        owner_z = jnp.bitwise_xor(z, d)
        _, core, part = group_of(owner_ref, owner_z * 2 + x)
        for s in range(2):
            source = 2 * jnp.bitwise_xor(x, s) + jnp.bitwise_xor(core, c)
            scale = scale_ref[source, pl.ds(pl.multiple_of(part * page, page), page), :]
            result = (keep_ref[owner_z, s] + came_ref[owner_z, s].astype(jnp.float32)) * scale
            if turn:
                cos_ref, sin_ref = refs[:2]
                result = result.astype(jnp.bfloat16).astype(jnp.float32)
                page_class = s * 4 + core * 2 + part
                turned = pltpu.roll(result, HD // 2, 1)
                result = result * cos_ref[page_class] + turned * sin_ref[page_class]
            out_ref[s * page : (s + 1) * page, :] = result.astype(jnp.bfloat16)


def finish(owner_map, keep, came, scale, *tables):
    line, _, page, _ = keep.shape
    return pl.pallas_call(
        functools.partial(finish_kernel, line, len(tables) > 0),
        in_specs=[SMEM] + [VMEM] * (3 + len(tables)),
        out_specs=[VMEM] * line,
        out_shape=[jax.ShapeDtypeStruct((2 * page, HD), jnp.bfloat16)] * line,
        compiler_params=pltpu.CompilerParams(vmem_limit_bytes=SMALL_VMEM_LIMIT),
    )(owner_map, keep, came, scale, *tables)


def place_kernel(*refs):
    out_ref = refs[-1]
    z = here()[2]
    rows = refs[0].shape[0]
    for d, block_ref in enumerate(refs[:-1]):
        start = pl.multiple_of(jnp.bitwise_xor(z, d) * rows, rows)
        out_ref[pl.ds(start, rows), :] = block_ref[...]


def place(blocks):
    return pl.pallas_call(
        place_kernel,
        in_specs=[VMEM] * len(blocks),
        out_specs=VMEM,
        out_shape=jax.ShapeDtypeStruct((len(blocks) * blocks[0].shape[0], HD), jnp.bfloat16),
        compiler_params=pltpu.CompilerParams(vmem_limit_bytes=SMALL_VMEM_LIMIT),
    )(*blocks)


def after(value, *others):
    return lax.optimization_barrier((value, *others))[0]


def paired_shards(hidden, gain_table, layer_id, w_key, w_value, offsets, owner_map):
    tok_count = lax.axis_size("tok")
    line = tok_count // 2
    _, x, _, _ = here()
    shard = w_key.shape[0]
    device_rows = hidden.shape[0]
    page = device_rows // 2

    def over_x(values):
        return lax.ppermute(values, "tok", [(t, t ^ 1) for t in range(tok_count)])

    def over_z(values, distance):
        return lax.ppermute(values, "tok", [(t, t ^ (2 * distance)) for t in range(tok_count)])

    def over_y(values):
        return lax.ppermute(values, "group", [(0, 1), (1, 0)])

    def over_c(values):
        return lax.ppermute(values, "col", [(0, 1), (1, 0)])

    other = over_c(hidden)
    away = away_half(hidden, shard)
    own_away = over_x(away)
    *pieces, packed = pack_weights(layer_id, after(w_key, away), w_value, gain_table)
    near_0 = over_z(pieces[0], 1)
    far_0 = over_z(pieces[0], 2)
    near_1 = over_z(after(pieces[1], other), 1)
    far_1 = over_z(after(pieces[1], near_0), 2)
    near_y_0 = over_y(near_0)

    wide = after(hidden, packed).astype(jnp.float32)
    own_squares = jnp.sum(wide * wide, axis=1)
    corner_0 = over_z(after(far_0, near_0, own_squares), 1)
    near_y_1 = over_y(near_1)
    far_y_0 = over_y(after(far_0, near_y_0))
    corner_1 = over_z(after(far_1, near_y_1), 1)
    far_y_1 = over_y(after(far_1, near_y_1))
    corner_y_0 = over_y(after(corner_0, far_y_0, corner_1))
    corner_y_1 = over_y(after(corner_1, far_y_1))
    start = jnp.broadcast_to(offsets[0].astype(jnp.float32), (device_rows,))
    own_facts = jnp.stack([own_squares, start])
    came_facts = over_x(after(own_facts, own_away))
    pair_facts = jnp.stack([own_facts, came_facts])
    other_away = over_c(after(own_away, corner_y_0, far_y_1, came_facts))

    starts = jnp.where(x == 0, pair_facts[:, 1, 0], pair_facts[::-1, 1, 0]).astype(jnp.int32)
    position = (starts[:, None] + jnp.arange(2 * device_rows, dtype=jnp.int32)).reshape(-1)
    cosine, sine = rotary_table(position, HD)
    cosine = jnp.concatenate([cosine, cosine], axis=1).reshape(8, page, HD)
    sine = jnp.concatenate([-sine, sine], axis=1).reshape(8, page, HD)
    pair_squares = pair_facts[:, 0]
    squares = jnp.stack([pair_squares, over_c(pair_squares)], axis=1).reshape(4, device_rows)
    scale = lax.rsqrt(squares / hidden.shape[1] + 1e-05)
    scale = jnp.broadcast_to(scale[:, :, None], (4, device_rows, HD))

    sources = [hidden, other, own_away, other_away]
    mine = [[packed], [near_0, near_1], [far_0, far_1], [corner_0, corner_1]]
    theirs = [[near_y_0, near_y_1], [far_y_0, far_y_1], [corner_y_0, corner_y_1]]
    key_keep, key_send = multiply(
        owner_map, sources, after(w_key, scale, cosine, sine), 0, mine, theirs
    )
    key_came = over_x(key_send)
    value_keep, value_send = multiply(
        owner_map, sources, after(w_value, key_send), 1, mine, theirs
    )
    value_came = over_x(value_send)
    keys = finish(owner_map, key_keep, key_came, scale, cosine, sine)
    values = finish(owner_map, value_keep, after(value_came, keys[0]), scale)
    keys = [keys[0]] + [over_z(keys[d], d) for d in range(1, line)]
    values = [values[0], after(values[1], *keys[1:]), *values[2:]]
    values = [values[0]] + [over_z(values[d], d) for d in range(1, line)]
    return (place(keys)[None], place(values)[None])


def solution(mesh):
    in_specs = (
        P(("group", "tok", "col"), None),
        P(None, "tok"),
        P("group"),
        P("tok", "col"),
        P("tok", "col"),
        P(("group", "tok")),
        P("group"),
    )
    out_specs = (P("col", ("group", "tok"), None), P("col", ("group", "tok"), None))
    paired = mesh.shape["group"] == 2 and mesh.shape["tok"] == 8 and mesh.shape["col"] == 2
    shards = paired_shards if paired else general_shards
    return jax.shard_map(shards, mesh=mesh, in_specs=in_specs, out_specs=out_specs, check_vma=False)
```

```python
import functools
import math

import jax
import jax.numpy as jnp
from jax import lax
from jax.experimental import pallas as pl
from jax.experimental.pallas import tpu as pltpu
from jax.sharding import PartitionSpec as P

HD = 128
GAIN_ROWS = 16
VMEM_LIMIT = 61 * 2**20
SMALL_VMEM_LIMIT = 8 * 2**20


def rotary_table(position, size_head):
    half_size = size_head // 2
    frequency = jnp.power(
        jnp.float32(500000.0), -2.0 * jnp.arange(half_size, dtype=jnp.float32) / size_head
    )
    angle = jnp.mod(position.astype(jnp.float32)[:, None] * frequency[None, :], 2.0 * math.pi)
    return jnp.cos(angle), jnp.sin(angle)


def rotate(unrotated, position):
    half_size = unrotated.shape[-1] // 2
    cosine, sine = rotary_table(position, unrotated.shape[-1])
    cosine, sine = cosine[:, None, :], sine[:, None, :]
    values = unrotated.astype(jnp.float32)
    first = values[..., :half_size]
    second = values[..., half_size:]
    return jnp.concatenate(
        [first * cosine - second * sine, second * cosine + first * sine], axis=-1
    ).astype(jnp.bfloat16)


def normalize(values, squares_total, gain, feature_count):
    scale = lax.rsqrt(squares_total / feature_count + 1e-05)
    return (values.astype(jnp.float32) * scale[:, None] * gain.astype(jnp.float32)[None, :]).astype(
        jnp.bfloat16
    )


def general_shards(hidden, gain_table, layer_id, w_key, w_value, offsets, owner_map):
    tok_count = lax.axis_size("tok")
    col_count = lax.axis_size("col")
    gain_piece = lax.dynamic_index_in_dim(gain_table, layer_id[0], 0, keepdims=False)
    gain_full = lax.all_gather(gain_piece, "tok", axis=0, tiled=True)
    feature_count = gain_full.shape[0]
    block_rows = hidden.shape[0] * col_count
    tok_rows = lax.all_gather(hidden, "col", axis=0, tiled=True)
    wide = tok_rows.astype(jnp.float32)
    normed = normalize(tok_rows, jnp.sum(wide * wide, axis=1), gain_full, feature_count)
    key_raw, value_new = (
        jnp.dot(
            normed,
            lax.all_gather(weight, "tok", axis=0, tiled=True),
            preferred_element_type=jnp.float32,
        ).astype(jnp.bfloat16)
        for weight in (w_key, w_value)
    )
    heads_here = key_raw.shape[1] // HD
    classes = tok_count // heads_here
    page = block_rows // classes
    group_ids = jnp.arange(tok_count, dtype=jnp.int32)
    inverse = jnp.zeros((tok_count,), jnp.int32).at[owner_map].set(group_ids)

    def arrange_pages(values):
        grouped = (
            values.reshape(classes, page, heads_here, HD)
            .transpose(2, 0, 1, 3)
            .reshape(tok_count, page, HD)
        )
        return jnp.take(grouped, inverse, axis=0).reshape(tok_count * page, HD)

    position = offsets[0] + jnp.arange(block_rows, dtype=jnp.int32)
    key_new = rotate(key_raw.reshape(block_rows, heads_here, HD), position).reshape(block_rows, -1)
    key_out, value_out = (
        lax.all_to_all(arrange_pages(values), "tok", split_axis=0, concat_axis=0, tiled=True)
        for values in (key_new, value_new)
    )
    return (key_out.reshape(1, -1, HD), value_out.reshape(1, -1, HD))


def run_copies(pairs, sems):
    copies = [
        pltpu.make_async_copy(source, target, sems.at[i])
        for i, (source, target) in enumerate(pairs)
    ]
    for copy in copies:
        copy.start()
    return copies


def wait_all(copies):
    for copy in copies:
        copy.wait()


SMEM = pl.BlockSpec(memory_space=pltpu.SMEM)
VMEM = pl.BlockSpec(memory_space=pltpu.VMEM)
HBM = pl.BlockSpec(memory_space=pltpu.HBM)


def here():
    tok = lax.axis_index("tok")
    return lax.axis_index("group"), tok % 2, tok // 2, lax.axis_index("col")


def half_kernel(shard, hidden_ref, half_ref, sems):
    x = here()[1]
    pairs = []
    for i in range(half_ref.shape[1] // shard):
        lanes = pl.ds(pl.multiple_of((2 * i + 1 - x) * shard, shard), shard)
        pairs.append((hidden_ref.at[:, lanes], half_ref.at[:, pl.ds(i * shard, shard)]))
    wait_all(run_copies(pairs, sems))


def away_half(hidden, shard):
    rows, features = hidden.shape
    return pl.pallas_call(
        functools.partial(half_kernel, shard),
        in_specs=[HBM],
        out_specs=VMEM,
        out_shape=jax.ShapeDtypeStruct((rows, features // 2), hidden.dtype),
        scratch_shapes=[pltpu.SemaphoreType.DMA((features // shard // 2,))],
        compiler_params=pltpu.CompilerParams(vmem_limit_bytes=SMALL_VMEM_LIMIT),
    )(hidden)


def pack_kernel(layer_ref, key_ref, value_ref, gain_ref, *refs):
    *packed_refs, table, sems = refs
    shard, columns = key_ref.shape
    half = shard // 2
    width = 2 * columns
    gain_parts = shard // width
    layer = layer_ref[0]
    block = pl.multiple_of(layer // GAIN_ROWS * GAIN_ROWS, GAIN_ROWS)
    pairs = [(gain_ref.at[pl.ds(block, GAIN_ROWS), :], table)]
    for i, packed_ref in enumerate(packed_refs):
        count = PACKED[i][1]
        rows = half // count
        first = pl.multiple_of(here()[0] * half + PACKED[i][0] * rows, rows)
        for k, weight_ref in enumerate((key_ref, value_ref)):
            target = packed_ref.at[pl.ds(0, rows), pl.ds(k * columns, columns)]
            pairs.append((weight_ref.at[pl.ds(first, rows), :], target))
    copies = run_copies(pairs, sems)
    copies[0].wait()
    found = table[...].astype(jnp.float32)
    pick = lax.broadcasted_iota(jnp.int32, found.shape, 0) == layer % GAIN_ROWS
    gain = jnp.sum(jnp.where(pick, found, 0.0), axis=0, keepdims=True)
    for i, packed_ref in enumerate(packed_refs):
        index, count = PACKED[i]
        rows = half // count
        for p in range(gain_parts // count):
            part = index * (gain_parts // count) + p
            packed_ref[rows + p * GAIN_ROWS : rows + (p + 1) * GAIN_ROWS, :] = jnp.broadcast_to(
                gain[:, part * width : (part + 1) * width], (GAIN_ROWS, width)
            ).astype(packed_ref.dtype)
    wait_all(copies[1:])


PACKED = ((0, 2), (1, 2), (0, 1))


def pack_weights(layer_id, w_key, w_value, gain_table):
    shard, columns = w_key.shape
    rows = shard // 2 + shard // (2 * columns) * GAIN_ROWS
    return pl.pallas_call(
        pack_kernel,
        in_specs=[SMEM, HBM, HBM, HBM],
        out_specs=[VMEM] * len(PACKED),
        out_shape=[
            jax.ShapeDtypeStruct((rows // count, 2 * columns), w_key.dtype) for _, count in PACKED
        ],
        scratch_shapes=[
            pltpu.VMEM((GAIN_ROWS, gain_table.shape[1]), gain_table.dtype),
            pltpu.SemaphoreType.DMA((1 + 2 * len(PACKED),)),
        ],
        compiler_params=pltpu.CompilerParams(vmem_limit_bytes=SMALL_VMEM_LIMIT),
    )(layer_id, w_key, w_value, gain_table)


def group_of(owner_ref, owner):
    group = jnp.int32(0)
    for g in range(owner_ref.shape[0]):
        group = jnp.where(owner_ref[g] == owner, g, group)
    return group // 4, group % 4 // 2, group % 2


def shard_pairs(d, mine, theirs, y, columns, picked, weights, gains):
    width = 2 * columns
    half = (mine[0].shape[0] - GAIN_ROWS * (2 // len(mine))) * len(mine)
    shard = 2 * half
    first = d * shard
    rows = half // len(mine)
    gain_parts = shard // width // len(mine)
    pairs = []
    for i, packed in enumerate(mine):
        for p in range(gain_parts):
            lanes = pl.ds(first + (i * gain_parts + p) * width, width)
            gain_rows = pl.ds(rows + p * GAIN_ROWS, GAIN_ROWS)
            pairs.append((packed.at[gain_rows, :], gains.at[:, lanes]))
    for blocks, side in ((mine if d > 0 else [], y), (theirs, 1 - y)):
        for i, packed in enumerate(blocks):
            start = pl.multiple_of(first + side * half + i * rows, rows)
            target = weights.at[pl.ds(start, rows), :]
            pairs.append((packed.at[pl.ds(0, rows), picked], target))
    return pairs


def early_kernel(shard, counts, *refs):
    refs = list(refs)
    sources = [refs.pop(0) for _ in range(2)]
    key_ref, value_ref = refs.pop(0), refs.pop(0)
    mine = [[refs.pop(0) for _ in range(count)] for count in counts]
    theirs = [[]] + [[refs.pop(0) for _ in range(count)] for count in counts[1:]]
    total, weights, gains, raw, sems = refs
    y, x, z, _ = here()
    columns = key_ref.shape[1]
    device_rows = sources[0].shape[0]
    pairs, ends = [], [0]
    for d in range(len(counts)):
        if d == 0:
            for k, weight_ref in enumerate((key_ref, value_ref)):
                target = weights.at[pl.ds(0, shard), pl.ds(k * columns, columns)]
                pairs.append((weight_ref, target))
        picked = pl.ds(0, 2 * columns)
        pairs += shard_pairs(d, mine[d], theirs[d], y, columns, picked, weights, gains)
        lanes = pl.ds(pl.multiple_of((2 * jnp.bitwise_xor(z, d) + x) * shard, shard), shard)
        for i, source in enumerate(sources):
            target = raw.at[pl.ds(i * device_rows, device_rows), pl.ds(d * shard, shard)]
            pairs.append((source.at[:, lanes], target))
        ends.append(len(pairs))
    copies = run_copies(pairs, sems)
    for d in range(len(counts)):
        wait_all(copies[ends[d] : ends[d + 1]])
        block = slice(d * shard, (d + 1) * shard)
        product = jnp.dot(
            raw[:, block] * gains[0:1, block], weights[block, :], preferred_element_type=jnp.float32
        )
        total[...] = product if d == 0 else total[...] + product


def early(sources, w_key, w_value, mine, theirs):
    shard, columns = w_key.shape
    counts = tuple(len(blocks) for blocks in mine)
    features = shard * len(mine)
    rows = 2 * sources[0].shape[0]
    operands = [
        *sources, w_key, w_value, *[packed for blocks in mine + theirs for packed in blocks],
    ]
    copies = len(mine) * (shard // (2 * columns) + 2) + 2 + 2 * sum(counts)
    return pl.pallas_call(
        functools.partial(early_kernel, shard, counts),
        in_specs=[HBM] * len(operands),
        out_specs=VMEM,
        out_shape=jax.ShapeDtypeStruct((rows, 2 * columns), jnp.float32),
        scratch_shapes=[
            pltpu.VMEM((features, 2 * columns), jnp.bfloat16),
            pltpu.VMEM((GAIN_ROWS, features), jnp.bfloat16),
            pltpu.VMEM((rows, features), jnp.bfloat16),
            pltpu.SemaphoreType.DMA((copies,)),
        ],
        compiler_params=pltpu.CompilerParams(vmem_limit_bytes=VMEM_LIMIT),
    )(*operands)


def multiply_kernel(shard, counts, which, *refs):
    refs = list(refs)
    owner_ref, before_ref = refs.pop(0), refs.pop(0)
    sources = [refs.pop(0) for _ in range(4)]
    weight_ref = refs.pop(0)
    line = len(counts)
    mine = [[refs.pop(0) for _ in range(count)] for count in counts]
    theirs = [[]] + [[refs.pop(0) for _ in range(count)] for count in counts[1:]]
    keep, send, weights, gains, raw, total, sems = refs
    y, x, z, c = here()
    columns = weight_ref.shape[1]
    _, _, page, _ = keep.shape
    device_rows = 2 * page
    picked = pl.ds(which * columns, columns)
    pairs, ends = [(before_ref.at[:, picked], total.at[pl.ds(0, 2 * device_rows), :])], []
    for d in range(line):
        first = d * shard
        if d == 0:
            pairs.append((weight_ref, weights.at[pl.ds(first, shard), :]))
        pairs += shard_pairs(d, mine[d], theirs[d], y, columns, picked, weights, gains)
        place_z = jnp.bitwise_xor(z, d)
        for i, source in enumerate(sources):
            if i < 2 and d < line - 1:
                continue
            block = 2 * place_z + x if i < 2 else place_z
            lanes = pl.ds(pl.multiple_of(block * shard, shard), shard)
            target = raw.at[pl.ds(i * device_rows, device_rows), pl.ds(first, shard)]
            pairs.append((source.at[:, lanes], target))
        ends.append(len(pairs))
    copies = run_copies(pairs, sems)
    for d in range(line):
        wait_all(copies[(ends[d - 1] if d > 0 else 0) : ends[d]])
        block = slice(d * shard, (d + 1) * shard)
        for i in range(0 if d == line - 1 else 1, 2):
            span = slice(i * 2 * device_rows, (i + 1) * 2 * device_rows)
            product = jnp.dot(
                raw[span, block] * gains[0:1, block],
                weights[block, :],
                preferred_element_type=jnp.float32,
            )
            total[span, :] = product if d == 0 else total[span, :] + product
    for owner_z in range(line):
        for owner_x, out in ((x, keep), (1 - x, send)):
            j, core, part = group_of(owner_ref, owner_z * 2 + owner_x)
            lanes = pl.ds(pl.multiple_of(j * HD, HD), HD)
            for side in range(2):
                source = 2 * side + jnp.bitwise_xor(core, c)
                start = pl.multiple_of(source * device_rows + part * page, page)
                out[owner_z, jnp.bitwise_xor(x, side)] = total[pl.ds(start, page), lanes].astype(
                    out.dtype
                )


def multiply(owner_map, before, sources, weight, which, mine, theirs):
    shard, columns = weight.shape
    line = len(mine)
    device_rows = sources[0].shape[0]
    operands = [
        before,
        *sources, weight,
        *[packed for blocks in mine + theirs for packed in blocks],
    ]
    shape = (line, 2, device_rows // 2, HD)
    counts = tuple(len(blocks) for blocks in mine)
    copies = 1 + line * (shard // (2 * columns)) + 1 + 2 * sum(counts) + 4 * line
    return pl.pallas_call(
        functools.partial(multiply_kernel, shard, counts, which),
        in_specs=[SMEM] + [HBM] * len(operands),
        out_specs=[VMEM] * 2,
        out_shape=[
            jax.ShapeDtypeStruct(shape, jnp.float32),
            jax.ShapeDtypeStruct(shape, jnp.bfloat16),
        ],
        scratch_shapes=[
            pltpu.VMEM((line * shard, columns), jnp.bfloat16),
            pltpu.VMEM((GAIN_ROWS, line * shard), jnp.bfloat16),
            pltpu.VMEM((4 * device_rows, line * shard), jnp.bfloat16),
            pltpu.VMEM((4 * device_rows, columns), jnp.float32),
            pltpu.SemaphoreType.DMA((copies,)),
        ],
        compiler_params=pltpu.CompilerParams(vmem_limit_bytes=VMEM_LIMIT),
    )(owner_map, *operands)


def finish_kernel(line, turn, owner_ref, keep_ref, came_ref, scale_ref, *refs):
    out_refs = refs[-line:]
    _, x, z, c = here()
    page = keep_ref.shape[2]
    for d, out_ref in enumerate(out_refs):
        owner_z = jnp.bitwise_xor(z, d)
        _, core, part = group_of(owner_ref, owner_z * 2 + x)
        for s in range(2):
            source = 2 * jnp.bitwise_xor(x, s) + jnp.bitwise_xor(core, c)
            scale = scale_ref[source, pl.ds(pl.multiple_of(part * page, page), page), :]
            result = (keep_ref[owner_z, s] + came_ref[owner_z, s].astype(jnp.float32)) * scale
            if turn:
                cos_ref, sin_ref = refs[:2]
                result = result.astype(jnp.bfloat16).astype(jnp.float32)
                page_class = s * 4 + core * 2 + part
                turned = pltpu.roll(result, HD // 2, 1)
                result = result * cos_ref[page_class] + turned * sin_ref[page_class]
            out_ref[s * page : (s + 1) * page, :] = result.astype(jnp.bfloat16)


def finish(owner_map, keep, came, scale, *tables):
    line, _, page, _ = keep.shape
    return pl.pallas_call(
        functools.partial(finish_kernel, line, len(tables) > 0),
        in_specs=[SMEM] + [VMEM] * (3 + len(tables)),
        out_specs=[VMEM] * line,
        out_shape=[jax.ShapeDtypeStruct((2 * page, HD), jnp.bfloat16)] * line,
        compiler_params=pltpu.CompilerParams(vmem_limit_bytes=SMALL_VMEM_LIMIT),
    )(owner_map, keep, came, scale, *tables)


def place_kernel(*refs):
    out_ref = refs[-1]
    z = here()[2]
    rows = refs[0].shape[0]
    for d, block_ref in enumerate(refs[:-1]):
        start = pl.multiple_of(jnp.bitwise_xor(z, d) * rows, rows)
        out_ref[pl.ds(start, rows), :] = block_ref[...]


def place(blocks):
    return pl.pallas_call(
        place_kernel,
        in_specs=[VMEM] * len(blocks),
        out_specs=VMEM,
        out_shape=jax.ShapeDtypeStruct((len(blocks) * blocks[0].shape[0], HD), jnp.bfloat16),
        compiler_params=pltpu.CompilerParams(vmem_limit_bytes=SMALL_VMEM_LIMIT),
    )(*blocks)


def after(value, *others):
    return lax.optimization_barrier((value, *others))[0]


def paired_shards(hidden, gain_table, layer_id, w_key, w_value, offsets, owner_map):
    tok_count = lax.axis_size("tok")
    line = tok_count // 2
    _, x, _, _ = here()
    shard = w_key.shape[0]
    device_rows = hidden.shape[0]
    page = device_rows // 2

    def over_x(values):
        return lax.ppermute(values, "tok", [(t, t ^ 1) for t in range(tok_count)])

    def over_z(values, distance):
        return lax.ppermute(values, "tok", [(t, t ^ (2 * distance)) for t in range(tok_count)])

    def over_y(values):
        return lax.ppermute(values, "group", [(0, 1), (1, 0)])

    def over_c(values):
        return lax.ppermute(values, "col", [(0, 1), (1, 0)])

    other = over_c(hidden)
    away = away_half(hidden, shard)
    own_away = over_x(away)
    *pieces, packed = pack_weights(layer_id, after(w_key, away), w_value, gain_table)
    near_0 = over_z(pieces[0], 1)
    far_0 = over_z(pieces[0], 2)
    near_1 = over_z(after(pieces[1], other), 1)
    far_1 = over_z(after(pieces[1], near_0), 2)
    near_y_0 = over_y(near_0)

    wide = after(hidden, packed).astype(jnp.float32)
    own_squares = jnp.sum(wide * wide, axis=1)
    corner_0 = over_z(after(far_0, near_0, own_squares), 1)
    near_y_1 = over_y(near_1)
    far_y_0 = over_y(after(far_0, near_y_0))
    corner_1 = over_z(after(far_1, near_y_1), 1)
    far_y_1 = over_y(after(far_1, near_y_1))
    corner_y_0 = over_y(after(corner_0, far_y_0, corner_1))
    corner_y_1 = over_y(after(corner_1, far_y_1))
    start = jnp.broadcast_to(offsets[0].astype(jnp.float32), (device_rows,))
    own_facts = jnp.stack([own_squares, start])
    came_facts = over_x(after(own_facts, own_away))
    pair_facts = jnp.stack([own_facts, came_facts])
    other_away = over_c(after(own_away, corner_y_0, far_y_1, came_facts))

    starts = jnp.where(x == 0, pair_facts[:, 1, 0], pair_facts[::-1, 1, 0]).astype(jnp.int32)
    position = (starts[:, None] + jnp.arange(2 * device_rows, dtype=jnp.int32)).reshape(-1)
    cosine, sine = rotary_table(position, HD)
    cosine = jnp.concatenate([cosine, cosine], axis=1).reshape(8, page, HD)
    sine = jnp.concatenate([-sine, sine], axis=1).reshape(8, page, HD)
    pair_squares = pair_facts[:, 0]
    squares = jnp.stack([pair_squares, over_c(pair_squares)], axis=1).reshape(4, device_rows)
    scale = lax.rsqrt(squares / hidden.shape[1] + 1e-05)
    scale = jnp.broadcast_to(scale[:, :, None], (4, device_rows, HD))

    sources = [hidden, other, own_away, other_away]
    mine = [[packed], [near_0, near_1], [far_0, far_1], [corner_0, corner_1]]
    theirs = [[near_y_0, near_y_1], [far_y_0, far_y_1], [corner_y_0, corner_y_1]]
    before = early([hidden, other], w_key, w_value, mine[:-1], theirs[:-1])
    key_keep, key_send = multiply(
        owner_map, before, sources, after(w_key, scale, cosine, sine), 0, mine, theirs
    )
    key_came = over_x(key_send)
    value_keep, value_send = multiply(
        owner_map, before, sources, after(w_value, key_send), 1, mine, theirs
    )
    value_came = over_x(value_send)
    keys = finish(owner_map, key_keep, key_came, scale, cosine, sine)
    values = finish(owner_map, value_keep, after(value_came, keys[0]), scale)
    keys = [keys[0]] + [over_z(keys[d], d) for d in range(1, line)]
    values = [values[0], after(values[1], *keys[1:]), *values[2:]]
    values = [values[0]] + [over_z(values[d], d) for d in range(1, line)]
    return (place(keys)[None], place(values)[None])


def solution(mesh):
    in_specs = (
        P(("group", "tok", "col"), None),
        P(None, "tok"),
        P("group"),
        P("tok", "col"),
        P("tok", "col"),
        P(("group", "tok")),
        P("group"),
    )
    out_specs = (P("col", ("group", "tok"), None), P("col", ("group", "tok"), None))
    paired = mesh.shape["group"] == 2 and mesh.shape["tok"] == 8 and mesh.shape["col"] == 2
    shards = paired_shards if paired else general_shards
    return jax.shard_map(shards, mesh=mesh, in_specs=in_specs, out_specs=out_specs, check_vma=False)
```

```python
import functools
import math

import jax
import jax.numpy as jnp
from jax import lax
from jax.experimental import pallas as pl
from jax.experimental.pallas import tpu as pltpu
from jax.sharding import PartitionSpec as P

HD = 128
GAIN_ROWS = 16
VMEM_LIMIT = 62 * 2**20
SMALL_VMEM_LIMIT = 8 * 2**20


def rotary_table(position, size_head):
    half_size = size_head // 2
    frequency = jnp.power(
        jnp.float32(500000.0), -2.0 * jnp.arange(half_size, dtype=jnp.float32) / size_head
    )
    angle = jnp.mod(position.astype(jnp.float32)[:, None] * frequency[None, :], 2.0 * math.pi)
    return jnp.cos(angle), jnp.sin(angle)


def rotate(unrotated, position):
    half_size = unrotated.shape[-1] // 2
    cosine, sine = rotary_table(position, unrotated.shape[-1])
    cosine, sine = cosine[:, None, :], sine[:, None, :]
    values = unrotated.astype(jnp.float32)
    first = values[..., :half_size]
    second = values[..., half_size:]
    return jnp.concatenate(
        [first * cosine - second * sine, second * cosine + first * sine], axis=-1
    ).astype(jnp.bfloat16)


def normalize(values, squares_total, gain, feature_count):
    scale = lax.rsqrt(squares_total / feature_count + 1e-05)
    return (values.astype(jnp.float32) * scale[:, None] * gain.astype(jnp.float32)[None, :]).astype(
        jnp.bfloat16
    )


def general_shards(hidden, gain_table, layer_id, w_key, w_value, offsets, owner_map):
    tok_count = lax.axis_size("tok")
    col_count = lax.axis_size("col")
    gain_piece = lax.dynamic_index_in_dim(gain_table, layer_id[0], 0, keepdims=False)
    gain_full = lax.all_gather(gain_piece, "tok", axis=0, tiled=True)
    feature_count = gain_full.shape[0]
    block_rows = hidden.shape[0] * col_count
    tok_rows = lax.all_gather(hidden, "col", axis=0, tiled=True)
    wide = tok_rows.astype(jnp.float32)
    normed = normalize(tok_rows, jnp.sum(wide * wide, axis=1), gain_full, feature_count)
    key_raw, value_new = (
        jnp.dot(
            normed,
            lax.all_gather(weight, "tok", axis=0, tiled=True),
            preferred_element_type=jnp.float32,
        ).astype(jnp.bfloat16)
        for weight in (w_key, w_value)
    )
    heads_here = key_raw.shape[1] // HD
    classes = tok_count // heads_here
    page = block_rows // classes
    group_ids = jnp.arange(tok_count, dtype=jnp.int32)
    inverse = jnp.zeros((tok_count,), jnp.int32).at[owner_map].set(group_ids)

    def arrange_pages(values):
        grouped = (
            values.reshape(classes, page, heads_here, HD)
            .transpose(2, 0, 1, 3)
            .reshape(tok_count, page, HD)
        )
        return jnp.take(grouped, inverse, axis=0).reshape(tok_count * page, HD)

    position = offsets[0] + jnp.arange(block_rows, dtype=jnp.int32)
    key_new = rotate(key_raw.reshape(block_rows, heads_here, HD), position).reshape(block_rows, -1)
    key_out, value_out = (
        lax.all_to_all(arrange_pages(values), "tok", split_axis=0, concat_axis=0, tiled=True)
        for values in (key_new, value_new)
    )
    return (key_out.reshape(1, -1, HD), value_out.reshape(1, -1, HD))


def run_copies(pairs, sems):
    copies = [
        pltpu.make_async_copy(source, target, sems.at[i])
        for i, (source, target) in enumerate(pairs)
    ]
    for copy in copies:
        copy.start()
    return copies


def wait_all(copies):
    for copy in copies:
        copy.wait()


SMEM = pl.BlockSpec(memory_space=pltpu.SMEM)
VMEM = pl.BlockSpec(memory_space=pltpu.VMEM)
HBM = pl.BlockSpec(memory_space=pltpu.HBM)


def here():
    tok = lax.axis_index("tok")
    return lax.axis_index("group"), tok % 2, tok // 2, lax.axis_index("col")


def half_kernel(shard, hidden_ref, half_ref, sems):
    x = here()[1]
    pairs = []
    for i in range(half_ref.shape[1] // shard):
        lanes = pl.ds(pl.multiple_of((2 * i + 1 - x) * shard, shard), shard)
        pairs.append((hidden_ref.at[:, lanes], half_ref.at[:, pl.ds(i * shard, shard)]))
    wait_all(run_copies(pairs, sems))


def away_half(hidden, shard):
    rows, features = hidden.shape
    return pl.pallas_call(
        functools.partial(half_kernel, shard),
        in_specs=[HBM],
        out_specs=VMEM,
        out_shape=jax.ShapeDtypeStruct((rows, features // 2), hidden.dtype),
        scratch_shapes=[pltpu.SemaphoreType.DMA((features // shard // 2,))],
        compiler_params=pltpu.CompilerParams(vmem_limit_bytes=SMALL_VMEM_LIMIT),
    )(hidden)


def pack_kernel(layer_ref, key_ref, value_ref, gain_ref, *refs):
    *packed_refs, table, sems = refs
    shard, columns = key_ref.shape
    half = shard // 2
    width = 2 * columns
    gain_parts = shard // width
    layer = layer_ref[0]
    block = pl.multiple_of(layer // GAIN_ROWS * GAIN_ROWS, GAIN_ROWS)
    pairs = [(gain_ref.at[pl.ds(block, GAIN_ROWS), :], table)]
    for i, packed_ref in enumerate(packed_refs):
        count = PACKED[i][1]
        rows = half // count
        first = pl.multiple_of(here()[0] * half + PACKED[i][0] * rows, rows)
        for k, weight_ref in enumerate((key_ref, value_ref)):
            target = packed_ref.at[pl.ds(0, rows), pl.ds(k * columns, columns)]
            pairs.append((weight_ref.at[pl.ds(first, rows), :], target))
    copies = run_copies(pairs, sems)
    copies[0].wait()
    found = table[...].astype(jnp.float32)
    pick = lax.broadcasted_iota(jnp.int32, found.shape, 0) == layer % GAIN_ROWS
    gain = jnp.sum(jnp.where(pick, found, 0.0), axis=0, keepdims=True)
    for i, packed_ref in enumerate(packed_refs):
        index, count = PACKED[i]
        rows = half // count
        for p in range(gain_parts // count):
            part = index * (gain_parts // count) + p
            packed_ref[rows + p * GAIN_ROWS : rows + (p + 1) * GAIN_ROWS, :] = jnp.broadcast_to(
                gain[:, part * width : (part + 1) * width], (GAIN_ROWS, width)
            ).astype(packed_ref.dtype)
    wait_all(copies[1:])


PACKED = ((0, 2), (1, 2), (0, 1))


def pack_weights(layer_id, w_key, w_value, gain_table):
    shard, columns = w_key.shape
    rows = shard // 2 + shard // (2 * columns) * GAIN_ROWS
    return pl.pallas_call(
        pack_kernel,
        in_specs=[SMEM, HBM, HBM, HBM],
        out_specs=[VMEM] * len(PACKED),
        out_shape=[
            jax.ShapeDtypeStruct((rows // count, 2 * columns), w_key.dtype) for _, count in PACKED
        ],
        scratch_shapes=[
            pltpu.VMEM((GAIN_ROWS, gain_table.shape[1]), gain_table.dtype),
            pltpu.SemaphoreType.DMA((1 + 2 * len(PACKED),)),
        ],
        compiler_params=pltpu.CompilerParams(vmem_limit_bytes=SMALL_VMEM_LIMIT),
    )(layer_id, w_key, w_value, gain_table)


def group_of(owner_ref, owner):
    group = jnp.int32(0)
    for g in range(owner_ref.shape[0]):
        group = jnp.where(owner_ref[g] == owner, g, group)
    return group // 4, group % 4 // 2, group % 2


def shard_pairs(d, mine, theirs, y, columns, picked, weights, gains):
    width = 2 * columns
    half = (mine[0].shape[0] - GAIN_ROWS * (2 // len(mine))) * len(mine)
    shard = 2 * half
    first = d * shard
    rows = half // len(mine)
    gain_parts = shard // width // len(mine)
    pairs = []
    for i, packed in enumerate(mine):
        for p in range(gain_parts):
            lanes = pl.ds(first + (i * gain_parts + p) * width, width)
            gain_rows = pl.ds(rows + p * GAIN_ROWS, GAIN_ROWS)
            pairs.append((packed.at[gain_rows, :], gains.at[:, lanes]))
    for blocks, side in ((mine if d > 0 else [], y), (theirs, 1 - y)):
        for i, packed in enumerate(blocks):
            start = pl.multiple_of(first + side * half + i * rows, rows)
            target = weights.at[pl.ds(start, rows), :]
            pairs.append((packed.at[pl.ds(0, rows), picked], target))
    return pairs


def early_kernel(shard, counts, *refs):
    refs = list(refs)
    sources = [refs.pop(0) for _ in range(2)]
    key_ref, value_ref = refs.pop(0), refs.pop(0)
    mine = [[refs.pop(0) for _ in range(count)] for count in counts]
    theirs = [[]] + [[refs.pop(0) for _ in range(count)] for count in counts[1:]]
    total, weights, gains, raw, sems = refs
    y, x, z, _ = here()
    columns = key_ref.shape[1]
    device_rows = sources[0].shape[0]
    pairs, ends = [], [0]
    for d in range(len(counts)):
        if d == 0:
            for k, weight_ref in enumerate((key_ref, value_ref)):
                target = weights.at[pl.ds(0, shard), pl.ds(k * columns, columns)]
                pairs.append((weight_ref, target))
        picked = pl.ds(0, 2 * columns)
        pairs += shard_pairs(d, mine[d], theirs[d], y, columns, picked, weights, gains)
        lanes = pl.ds(pl.multiple_of((2 * jnp.bitwise_xor(z, d) + x) * shard, shard), shard)
        for i, source in enumerate(sources):
            target = raw.at[pl.ds(i * device_rows, device_rows), pl.ds(d * shard, shard)]
            pairs.append((source.at[:, lanes], target))
        ends.append(len(pairs))
    copies = run_copies(pairs, sems)
    for d in range(len(counts)):
        wait_all(copies[ends[d] : ends[d + 1]])
        block = slice(d * shard, (d + 1) * shard)
        product = jnp.dot(
            raw[:, block] * gains[0:1, block], weights[block, :], preferred_element_type=jnp.float32
        )
        total[...] = product if d == 0 else total[...] + product


def early(sources, w_key, w_value, mine, theirs):
    shard, columns = w_key.shape
    counts = tuple(len(blocks) for blocks in mine)
    features = shard * len(mine)
    rows = 2 * sources[0].shape[0]
    operands = [
        *sources, w_key, w_value, *[packed for blocks in mine + theirs for packed in blocks],
    ]
    copies = len(mine) * (shard // (2 * columns) + 2) + 2 + 2 * sum(counts)
    return pl.pallas_call(
        functools.partial(early_kernel, shard, counts),
        in_specs=[HBM] * len(operands),
        out_specs=VMEM,
        out_shape=jax.ShapeDtypeStruct((rows, 2 * columns), jnp.float32),
        scratch_shapes=[
            pltpu.VMEM((features, 2 * columns), jnp.bfloat16),
            pltpu.VMEM((GAIN_ROWS, features), jnp.bfloat16),
            pltpu.VMEM((rows, features), jnp.bfloat16),
            pltpu.SemaphoreType.DMA((copies,)),
        ],
        compiler_params=pltpu.CompilerParams(vmem_limit_bytes=VMEM_LIMIT),
    )(*operands)


def multiply_kernel(shard, counts, which, *refs):
    refs = list(refs)
    owner_ref, before_ref = refs.pop(0), refs.pop(0)
    sources = [refs.pop(0) for _ in range(4)]
    weight_ref = refs.pop(0)
    line = len(counts)
    mine = [[refs.pop(0) for _ in range(count)] for count in counts]
    theirs = [[]] + [[refs.pop(0) for _ in range(count)] for count in counts[1:]]
    keep, send, weights, gains, raw, total, sems = refs
    y, x, z, c = here()
    columns = weight_ref.shape[1]
    _, _, page, _ = keep.shape
    device_rows = 2 * page
    picked = pl.ds(which * columns, columns)
    pairs, ends = [(before_ref.at[:, picked], total.at[pl.ds(0, 2 * device_rows), :])], []
    for d in range(line):
        first = d * shard
        if d == 0:
            pairs.append((weight_ref, weights.at[pl.ds(first, shard), :]))
        pairs += shard_pairs(d, mine[d], theirs[d], y, columns, picked, weights, gains)
        place_z = jnp.bitwise_xor(z, d)
        for i, source in enumerate(sources):
            if i < 2 and d < line - 1:
                continue
            block = 2 * place_z + x if i < 2 else place_z
            lanes = pl.ds(pl.multiple_of(block * shard, shard), shard)
            target = raw.at[pl.ds(i * device_rows, device_rows), pl.ds(first, shard)]
            pairs.append((source.at[:, lanes], target))
        ends.append(len(pairs))
    copies = run_copies(pairs, sems)
    for d in range(line):
        wait_all(copies[(ends[d - 1] if d > 0 else 0) : ends[d]])
        block = slice(d * shard, (d + 1) * shard)
        for i in range(0 if d == line - 1 else 1, 2):
            span = slice(i * 2 * device_rows, (i + 1) * 2 * device_rows)
            product = jnp.dot(
                raw[span, block] * gains[0:1, block],
                weights[block, :],
                preferred_element_type=jnp.float32,
            )
            total[span, :] = product if d == 0 else total[span, :] + product
    for owner_z in range(line):
        for owner_x, out in ((x, keep), (1 - x, send)):
            j, core, part = group_of(owner_ref, owner_z * 2 + owner_x)
            lanes = pl.ds(pl.multiple_of(j * HD, HD), HD)
            for side in range(2):
                source = 2 * side + jnp.bitwise_xor(core, c)
                start = pl.multiple_of(source * device_rows + part * page, page)
                out[owner_z, jnp.bitwise_xor(x, side)] = total[pl.ds(start, page), lanes].astype(
                    out.dtype
                )


def multiply(owner_map, before, sources, weight, which, mine, theirs):
    shard, columns = weight.shape
    line = len(mine)
    device_rows = sources[0].shape[0]
    operands = [
        before,
        *sources, weight,
        *[packed for blocks in mine + theirs for packed in blocks],
    ]
    shape = (line, 2, device_rows // 2, HD)
    counts = tuple(len(blocks) for blocks in mine)
    copies = 1 + line * (shard // (2 * columns)) + 1 + 2 * sum(counts) + 4 * line
    return pl.pallas_call(
        functools.partial(multiply_kernel, shard, counts, which),
        in_specs=[SMEM] + [HBM] * len(operands),
        out_specs=[VMEM] * 2,
        out_shape=[
            jax.ShapeDtypeStruct(shape, jnp.float32),
            jax.ShapeDtypeStruct(shape, jnp.bfloat16),
        ],
        scratch_shapes=[
            pltpu.VMEM((line * shard, columns), jnp.bfloat16),
            pltpu.VMEM((GAIN_ROWS, line * shard), jnp.bfloat16),
            pltpu.VMEM((4 * device_rows, line * shard), jnp.bfloat16),
            pltpu.VMEM((4 * device_rows, columns), jnp.float32),
            pltpu.SemaphoreType.DMA((copies,)),
        ],
        compiler_params=pltpu.CompilerParams(vmem_limit_bytes=VMEM_LIMIT),
    )(owner_map, *operands)


def finish_kernel(line, turn, owner_ref, keep_ref, came_ref, scale_ref, *refs):
    out_refs = refs[-line:]
    _, x, z, c = here()
    page = keep_ref.shape[2]
    for d, out_ref in enumerate(out_refs):
        owner_z = jnp.bitwise_xor(z, d)
        _, core, part = group_of(owner_ref, owner_z * 2 + x)
        for s in range(2):
            source = 2 * jnp.bitwise_xor(x, s) + jnp.bitwise_xor(core, c)
            scale = scale_ref[source, pl.ds(pl.multiple_of(part * page, page), page), :]
            result = (keep_ref[owner_z, s] + came_ref[owner_z, s].astype(jnp.float32)) * scale
            if turn:
                cos_ref, sin_ref = refs[:2]
                result = result.astype(jnp.bfloat16).astype(jnp.float32)
                page_class = s * 4 + core * 2 + part
                turned = pltpu.roll(result, HD // 2, 1)
                result = result * cos_ref[page_class] + turned * sin_ref[page_class]
            out_ref[s * page : (s + 1) * page, :] = result.astype(jnp.bfloat16)


def finish(owner_map, keep, came, scale, *tables):
    line, _, page, _ = keep.shape
    return pl.pallas_call(
        functools.partial(finish_kernel, line, len(tables) > 0),
        in_specs=[SMEM] + [VMEM] * (3 + len(tables)),
        out_specs=[VMEM] * line,
        out_shape=[jax.ShapeDtypeStruct((2 * page, HD), jnp.bfloat16)] * line,
        compiler_params=pltpu.CompilerParams(vmem_limit_bytes=SMALL_VMEM_LIMIT),
    )(owner_map, keep, came, scale, *tables)


def place_kernel(*refs):
    out_ref = refs[-1]
    z = here()[2]
    rows = refs[0].shape[0]
    for d, block_ref in enumerate(refs[:-1]):
        start = pl.multiple_of(jnp.bitwise_xor(z, d) * rows, rows)
        out_ref[pl.ds(start, rows), :] = block_ref[...]


def place(blocks):
    return pl.pallas_call(
        place_kernel,
        in_specs=[VMEM] * len(blocks),
        out_specs=VMEM,
        out_shape=jax.ShapeDtypeStruct((len(blocks) * blocks[0].shape[0], HD), jnp.bfloat16),
        compiler_params=pltpu.CompilerParams(vmem_limit_bytes=SMALL_VMEM_LIMIT),
    )(*blocks)


def after(value, *others):
    return lax.optimization_barrier((value, *others))[0]


def paired_shards(hidden, gain_table, layer_id, w_key, w_value, offsets, owner_map):
    tok_count = lax.axis_size("tok")
    line = tok_count // 2
    _, x, _, _ = here()
    shard = w_key.shape[0]
    device_rows = hidden.shape[0]
    page = device_rows // 2

    def over_x(values):
        return lax.ppermute(values, "tok", [(t, t ^ 1) for t in range(tok_count)])

    def over_z(values, distance):
        return lax.ppermute(values, "tok", [(t, t ^ (2 * distance)) for t in range(tok_count)])

    def over_y(values):
        return lax.ppermute(values, "group", [(0, 1), (1, 0)])

    def over_c(values):
        return lax.ppermute(values, "col", [(0, 1), (1, 0)])

    other = over_c(hidden)
    away = away_half(hidden, shard)
    own_away = over_x(away)
    *pieces, packed = pack_weights(layer_id, after(w_key, away), w_value, gain_table)
    near_0 = over_z(pieces[0], 1)
    far_0 = over_z(pieces[0], 2)
    near_1 = over_z(after(pieces[1], other), 1)
    far_1 = over_z(after(pieces[1], near_0), 2)
    near_y_0 = over_y(near_0)

    wide = after(hidden, packed).astype(jnp.float32)
    own_squares = jnp.sum(wide * wide, axis=1)
    corner_0 = over_z(after(far_0, near_0, own_squares), 1)
    near_y_1 = over_y(near_1)
    far_y_0 = over_y(after(far_0, near_y_0))
    corner_1 = over_z(after(far_1, near_y_1), 1)
    far_y_1 = over_y(after(far_1, near_y_1))
    corner_y_0 = over_y(after(corner_0, far_y_0, corner_1))
    corner_y_1 = over_y(after(corner_1, far_y_1))
    start = jnp.broadcast_to(offsets[0].astype(jnp.float32), (device_rows,))
    own_facts = jnp.stack([own_squares, start])
    came_facts = over_x(after(own_facts, own_away))
    pair_facts = jnp.stack([own_facts, came_facts])
    other_away = over_c(after(own_away, corner_y_0, far_y_1, came_facts))

    starts = jnp.where(x == 0, pair_facts[:, 1, 0], pair_facts[::-1, 1, 0]).astype(jnp.int32)
    position = (starts[:, None] + jnp.arange(2 * device_rows, dtype=jnp.int32)).reshape(-1)
    cosine, sine = rotary_table(position, HD)
    cosine = jnp.concatenate([cosine, cosine], axis=1).reshape(8, page, HD)
    sine = jnp.concatenate([-sine, sine], axis=1).reshape(8, page, HD)
    pair_squares = pair_facts[:, 0]
    squares = jnp.stack([pair_squares, over_c(pair_squares)], axis=1).reshape(4, device_rows)
    scale = lax.rsqrt(squares / hidden.shape[1] + 1e-05)
    scale = jnp.broadcast_to(scale[:, :, None], (4, device_rows, HD))

    sources = [hidden, other, own_away, other_away]
    mine = [[packed], [near_0, near_1], [far_0, far_1], [corner_0, corner_1]]
    theirs = [[near_y_0, near_y_1], [far_y_0, far_y_1], [corner_y_0, corner_y_1]]
    before = early([hidden, other], w_key, w_value, mine[:-1], theirs[:-1])
    key_keep, key_send = multiply(
        owner_map, before, sources, after(w_key, scale, cosine, sine), 0, mine, theirs
    )
    key_came = over_x(key_send)
    value_keep, value_send = multiply(
        owner_map, before, sources, after(w_value, key_send), 1, mine, theirs
    )
    value_came = over_x(value_send)
    keys = finish(owner_map, key_keep, key_came, scale, cosine, sine)
    values = finish(owner_map, value_keep, after(value_came, keys[0]), scale)
    keys = [keys[0]] + [over_z(keys[d], d) for d in range(1, line)]
    values = [values[0], after(values[1], *keys[1:]), *values[2:]]
    values = [values[0]] + [over_z(values[d], d) for d in range(1, line)]
    return (place(keys)[None], place(values)[None])


def solution(mesh):
    in_specs = (
        P(("group", "tok", "col"), None),
        P(None, "tok"),
        P("group"),
        P("tok", "col"),
        P("tok", "col"),
        P(("group", "tok")),
        P("group"),
    )
    out_specs = (P("col", ("group", "tok"), None), P("col", ("group", "tok"), None))
    paired = mesh.shape["group"] == 2 and mesh.shape["tok"] == 8 and mesh.shape["col"] == 2
    shards = paired_shards if paired else general_shards
    return jax.shard_map(shards, mesh=mesh, in_specs=in_specs, out_specs=out_specs, check_vma=False)
```
